32 devices in a mesh: gx: 4 (over z), yz: 8 (over y, x, core).
Axes of the slice: x: 2, y: 2, z: 4, core: 2. Of those that a mesh axis runs over, the one named last changes fastest.
Arguments:
- camera_accel: float32 [4, 1024, 3, 16, 128], P('gx', 'yz'), may hold values from -8 to 8
- camera_weight: float32 [4, 1024, 16, 128], P('gx', 'yz'), may hold values from 0.25 to 4
- brick_slot: int32 [4, 1024], P('gx', 'yz'), may hold values from 0 to 1023, as said below
- brick_solid: int32 [4, 1024], P('gx', 'yz'), may hold values from 0 to 1, as said below
Outputs:
- solution: float32 [8, 1024, 1024], P('yz', 'gx')
- residual: float32 [8, 1024, 1024], P('yz', 'gx')
The draws below stay inside these ranges and needn't reach their ends.
Inputs may be any that keep to these rules, and one draw needn't show every extreme that they name: `brick_slot`: row g lists each in-slab brick number of slab g once; entries j * 128 to (j + 1) * 128 - 1 are the bricks that camera owner j holds; brick number i belongs to solver owner i // 128. One camera owner holds at most 24 bricks of one solver owner, and exactly 24 of some in every slab. `brick_solid`: 1 marks a solid brick, numbered as in brick_slot; every slab has solid and fluid bricks.
All inputs are finite; a program needn't handle non-finite values.
Results may differ from the reference program's by a relative error of at most 0.00024.
Values sent between devices are 32-bit elements; how exact they have to be, the bound alone decides.
A program may use at most 128 MiB of HBM per device.

```python
import math
import jax
import jax.numpy as jnp
from jax import lax

NX = 1024
NY = 1024
ZL = 1
BR = 16
B = 128
ITERS = 2
XL = 256
NZ = 8
BPD = 128
N_GX = 4
N_YZ = 8


def draw_camera_accel(key, part):
    shape = (N_GX, N_YZ * BPD, 3, ZL * BR, B)
    values = jax.random.normal(key, shape, jnp.float32)
    return jnp.clip(values, -8.0, 8.0)


def draw_brick_slot(key, part):
    owner_count = N_YZ
    slot_count = BPD
    base_load = slot_count // owner_count
    swing = base_load // 2

    def shuffle_slots(owner_key):
        return jax.random.permutation(owner_key, slot_count).astype(jnp.int32)

    def one_slab(slab_key):
        split_keys = jax.random.split(slab_key, 3)
        raised = jax.random.permutation(split_keys[0], owner_count).astype(jnp.int32)
        lowered = jnp.roll(raised, -1)
        owner_ids = jnp.arange(owner_count, dtype=jnp.int32)
        counts = base_load + swing * (raised[:, None] == owner_ids[None, :]).astype(jnp.int32)
        counts = counts - swing * (lowered[:, None] == owner_ids[None, :]).astype(jnp.int32)
        start_owner = jnp.cumsum(counts, axis=0) - counts
        end_camera = jnp.cumsum(counts, axis=1)
        start_camera = end_camera - counts
        local_order = jax.vmap(shuffle_slots)(jax.random.split(split_keys[1], owner_count))
        slot_ids = jnp.arange(slot_count, dtype=jnp.int32)
        owner_of = jnp.sum((end_camera[:, None, :] <= slot_ids[None, :, None]).astype(jnp.int32), axis=2)
        within = slot_ids[None, :] - jnp.take_along_axis(start_camera, owner_of, axis=1)
        offset = jnp.take_along_axis(start_owner, owner_of, axis=1) + within
        local_ids = local_order[owner_of, offset]
        brick_ids = owner_of * slot_count + local_ids
        camera_perm = jax.vmap(shuffle_slots)(jax.random.split(split_keys[2], owner_count))
        brick_ids = jnp.take_along_axis(brick_ids, camera_perm, axis=1)
        return brick_ids.reshape(owner_count * slot_count).astype(jnp.int32)
    return jax.vmap(one_slab)(jax.random.split(key, N_GX))


def draw_brick_solid(key, part):
    x_bricks = NX // N_GX // BR
    y_bricks = NY // B
    z_span = max(1, N_YZ // 2)
    x_span = max(1, x_bricks // 2)
    y_span = max(1, y_bricks // 2)

    def one_slab(slab_key):
        split_keys = jax.random.split(slab_key, 3)
        z_first = jax.random.randint(split_keys[0], (), 0, N_YZ - z_span + 1)
        x_first = jax.random.randint(split_keys[1], (), 0, x_bricks - x_span + 1)
        y_first = jax.random.randint(split_keys[2], (), 0, y_bricks - y_span + 1)
        brick_ids = jnp.arange(N_YZ * BPD, dtype=jnp.int32)
        z_brick = brick_ids // BPD
        x_brick = brick_ids % BPD // y_bricks
        y_brick = brick_ids % y_bricks
        inside = (z_brick >= z_first) & (z_brick < z_first + z_span)
        inside = inside & (x_brick >= x_first) & (x_brick < x_first + x_span)
        inside = inside & (y_brick >= y_first) & (y_brick < y_first + y_span)
        return inside.astype(jnp.int32)
    return jax.vmap(one_slab)(jax.random.split(key, N_GX))


def block_scale(stream_key, dims, cuts, low, high):
    loudness, own = 1.0, jax.random.fold_in(stream_key, 6)
    for dim, shards_of in cuts:
        heights = jnp.exp(jax.random.uniform(jax.random.fold_in(own, dim), (shards_of,), jnp.float32, low / len(cuts), high / len(cuts)))
        loudness = loudness * jnp.repeat(heights, dims[dim] // shards_of).reshape([-1 if axis == dim else 1 for axis in range(len(dims))])
    return loudness


def setup_inputs(seed: int = 0) -> dict:
    seeds = jax.random.split(jax.random.key(seed), 5)
    return {
        "camera_accel": draw_camera_accel(jax.random.fold_in(seeds[4], 71), 0),
        "camera_weight": jnp.clip(jnp.exp(math.log(4.0) - 2.7725887 * jax.random.uniform(seeds[1], (N_GX, N_YZ * BPD, ZL * BR, B), jnp.float32) ** block_scale(seeds[1], (N_GX, N_YZ * BPD, ZL * BR, B), ((0, 4), (1, 8)), -0.2, 0.2)), 0.25, 4.0),
        "brick_slot": draw_brick_slot(jax.random.fold_in(seeds[4], 71), 0),
        "brick_solid": draw_brick_solid(jax.random.fold_in(seeds[4], 71), 0),
    }


shift_rate = 0.05
spectral_gain = 1.0
spectral_floor = 2.0
highest = lax.Precision.HIGHEST

def cosine_table(length, row_start, row_count, col_start, col_count):
    row_ids = row_start + jnp.arange(row_count, dtype=jnp.int32)
    col_ids = col_start + jnp.arange(col_count, dtype=jnp.int32)
    phases = jnp.remainder(row_ids[:, None] * (2 * col_ids[None, :] + 1), 4 * length).astype(jnp.float32)
    angles = phases * (jnp.pi / (2.0 * length))
    norm_scale = jnp.where(row_ids == 0, 1.0 / length, 2.0 / length).astype(jnp.float32)
    return jnp.sqrt(norm_scale)[:, None] * jnp.cos(angles)

def eigen_values(length, first_mode, mode_count):
    modes = (first_mode + jnp.arange(mode_count, dtype=jnp.int32)).astype(jnp.float32)
    return 2.0 - 2.0 * jnp.cos(modes * (jnp.pi / length))

def to_grid(bricks):
    channels = bricks.shape[2]
    shaped = bricks.reshape(N_GX, N_YZ, XL // BR, NY // B, channels, ZL, BR, B)
    shaped = jnp.transpose(shaped, (4, 1, 5, 0, 2, 6, 3, 7))
    return shaped.reshape(channels, NZ, NX, NY)

def next_cell(values_in, axis_index):
    padding = [(0, 0), (0, 0), (0, 0)]
    padding[axis_index] = (0, 1)
    return lax.slice_in_dim(jnp.pad(values_in, padding), 1, values_in.shape[axis_index] + 1, axis=axis_index)

def prev_cell(values_in, axis_index):
    padding = [(0, 0), (0, 0), (0, 0)]
    padding[axis_index] = (1, 0)
    return lax.slice_in_dim(jnp.pad(values_in, padding), 0, values_in.shape[axis_index], axis=axis_index)

def reference(camera_accel, camera_weight, brick_slot, brick_solid):
    fluid_bricks = (1 - brick_solid).astype(jnp.float32)

    def place(values_in, brick_ids):
        return jnp.zeros_like(values_in).at[brick_ids].set(values_in)
    brick_mask = fluid_bricks[:, :, None, None, None]
    accel = to_grid(jax.vmap(place)(camera_accel, brick_slot) * brick_mask)
    weight = to_grid(jax.vmap(place)(camera_weight[:, :, None], brick_slot) * brick_mask)[0]
    fluid = to_grid(jnp.broadcast_to(brick_mask, (N_GX, N_YZ * BPD, 1, ZL * BR, B)))[0]
    face_list = []
    for axis_index in range(3):
        face_list.append(jnp.sqrt(weight * next_cell(weight, axis_index)))
    diagonal = shift_rate * weight + (1.0 - fluid)
    source_term = jnp.zeros_like(weight)
    for axis_index in range(3):
        face_flux = face_list[axis_index] * (accel[axis_index] + next_cell(accel[axis_index], axis_index)) * 0.5
        source_term = source_term + prev_cell(face_flux, axis_index) - face_flux
        diagonal = diagonal + face_list[axis_index] + prev_cell(face_list[axis_index], axis_index)

    def operate(values_in):
        result = diagonal * values_in
        for axis_index in range(3):
            result = result - face_list[axis_index] * next_cell(values_in, axis_index)
            result = result - prev_cell(face_list[axis_index], axis_index) * prev_cell(values_in, axis_index)
        return result
    table_x = cosine_table(NX, 0, NX, 0, NX)
    table_y = cosine_table(NY, 0, NY, 0, NY)
    denom = spectral_gain * (eigen_values(NX, 0, NX)[:, None] + eigen_values(NY, 0, NY)[None, :]) + spectral_floor

    def precondition(values_in):
        spectrum = jnp.einsum('zxy,ky->zxk', values_in, table_y, precision=highest)
        spectrum = jnp.einsum('kx,zxy->zky', table_x, spectrum, precision=highest)
        spectrum = spectrum / denom[None]
        spatial = jnp.einsum('kx,zky->zxy', table_x, spectrum, precision=highest)
        spatial = jnp.einsum('zxk,ky->zxy', spatial, table_y, precision=highest)
        return fluid * spatial
    solution = jnp.zeros_like(source_term)
    residual = source_term
    update = precondition(residual)
    energy_now = jnp.sum(residual * update)
    direction = update
    for step_index in range(ITERS):
        image_of = operate(direction)
        step_size = energy_now / jnp.sum(direction * image_of)
        solution = solution + step_size * direction
        residual = residual - step_size * image_of
        if step_index + 1 < ITERS:
            update = precondition(residual)
            energy_next = jnp.sum(residual * update)
            direction = update + energy_next / energy_now * direction
            energy_now = energy_next
    return (solution, residual)
```

```python
import functools

import jax
import jax.numpy as jnp
import ml_dtypes
import numpy as np
from jax import lax
from jax.experimental import pallas as pl
from jax.experimental.pallas import tpu as pltpu
from jax.sharding import PartitionSpec as P

NX = 1024
NY = 1024
BR = 16
B = 128
ITERS = 2

shift_rate = 0.05
spectral_gain = 1.0
spectral_floor = 2.0

MESH = pl.DeviceIdType.MESH
PAD = 8
CHUNK = 16
TILE = 256


def cosine_table(length):
    rows = np.arange(length, dtype=np.int64)[:, None]
    cols = np.arange(length, dtype=np.int64)[None, :]
    phases = (rows * (2 * cols + 1)) % (4 * length)
    scale = np.sqrt(np.where(rows == 0, 1.0, 2.0) / length)
    return scale * np.cos(phases * (np.pi / (2.0 * length)))


def eigen_values(length):
    return 2.0 - 2.0 * np.cos(np.arange(length) * (np.pi / length))


def high_low(table):
    high = table.astype(np.float32).astype(ml_dtypes.bfloat16)
    low = (table - high.astype(np.float64)).astype(np.float32).astype(ml_dtypes.bfloat16)
    return np.stack([high, low])


def solver_tables(slabs, rows):
    table_y = cosine_table(NY)
    table_x = cosine_table(rows)
    inverse = 1.0 / (
        spectral_gain * (eigen_values(rows)[:, None] + eigen_values(NY)[None, :]) + spectral_floor
    )
    first, last = table_x[:, :1], table_x[:, -1:]
    same = np.sum(first * first * inverse, axis=0)
    cross = np.sum(first * last * inverse, axis=0)
    faces = slabs - 1
    couple = np.zeros((slabs, 2, 2 * slabs, NY))
    if faces:
        matrix = np.zeros((NY, faces, faces))
        for i in range(faces):
            matrix[:, i, i] = 1.0 / spectral_gain + 2.0 * same
            if i:
                matrix[:, i, i - 1] = matrix[:, i - 1, i] = -cross
        solved = np.linalg.inv(matrix)
        for slab in range(slabs):
            for side, face, sign in ((0, slab - 1, 1.0), (1, slab, -1.0)):
                if 0 <= face < faces:
                    for other in range(faces):
                        couple[slab, side, 2 * other + 1] += sign * solved[:, face, other]
                        couple[slab, side, 2 * other + 2] -= sign * solved[:, face, other]
    ends = np.concatenate([np.repeat(first, B, 1), np.repeat(last, B, 1)], axis=1)
    return (
        high_low(table_y.T),
        high_low(table_y),
        high_low(table_x),
        high_low(table_x.T),
        inverse.astype(np.float32),
        ends.astype(np.float32),
        couple.astype(np.float32),
    )


def exchange_kernel(owners, per_owner, src_ref, accel_ref, weight_ref, out_ref, send, send_sem, recv_sem):
    me = lax.axis_index("yz")
    barrier = pltpu.get_barrier_semaphore()
    for k in range(1, owners):
        pl.semaphore_signal(
            barrier, inc=1, device_id={"yz": lax.rem(me + k, owners)}, device_id_type=MESH
        )
    pl.semaphore_wait(barrier, owners - 1)

    def pack(k, owner):
        def one(p, carry):
            slot = src_ref[owner * per_owner + p]
            send[k, p, 0] = weight_ref[slot]
            send[k, p, 1] = accel_ref[slot, 0]
            send[k, p, 2] = accel_ref[slot, 1]
            send[k, p, 3] = accel_ref[slot, 2]
            return carry

        lax.fori_loop(0, per_owner, one, 0)

    copies = []
    for k in range(1, owners):
        owner = lax.rem(me + k, owners)
        pack(k, owner)
        copy = pltpu.make_async_remote_copy(
            src_ref=send.at[k],
            dst_ref=out_ref.at[me],
            send_sem=send_sem.at[k],
            recv_sem=recv_sem.at[k],
            device_id={"yz": owner},
            device_id_type=MESH,
        )
        copy.start()
        copies.append(copy)
    pack(0, me)
    own = pltpu.make_async_copy(send.at[0], out_ref.at[me], send_sem.at[0])
    own.start()
    own.wait()
    for copy in copies:
        copy.wait()


def exchange(source, accel, weight, owners, per_owner):
    slots, _, row_cells, col_cells = accel.shape
    shape = (owners, per_owner, 4, row_cells, col_cells)
    return pl.pallas_call(
        functools.partial(exchange_kernel, owners, per_owner),
        out_shape=jax.ShapeDtypeStruct(shape, jnp.float32),
        in_specs=[
            pl.BlockSpec(memory_space=pltpu.SMEM),
            pl.BlockSpec(memory_space=pltpu.VMEM),
            pl.BlockSpec(memory_space=pltpu.VMEM),
        ],
        out_specs=pl.BlockSpec(memory_space=pl.ANY),
        scratch_shapes=[
            pltpu.VMEM(shape, jnp.float32),
            pltpu.SemaphoreType.DMA((owners,)),
            pltpu.SemaphoreType.DMA((owners,)),
        ],
        compiler_params=pltpu.CompilerParams(
            collective_id=0, has_side_effects=True, vmem_limit_bytes=40 * 2**20
        ),
        name="brick_exchange",
    )(source, accel, weight)


def split(value):
    high = value.astype(jnp.bfloat16)
    return high, (value - high.astype(jnp.float32)).astype(jnp.bfloat16)


def dot32(left, right):
    return jnp.dot(left, right, preferred_element_type=jnp.float32)


def solver_kernel(
    slabs, owners, rows, y_bricks,
    anchor_ref, fluid_ref, bricks_ref, fwd_hbm, inv_hbm, table_x, table_xt, inverse_ref, ends_ref, couple_ref,
    solution_ref, residual_ref,
    fwd, inv, root, accel_x, accel_y, accel_z, fluid, diagonal, near_root, near_accel, near_t, t_pad,
    res_hl, spec, x_hl, update, image, edge, gathered, part, total_yz, total_gx,
    table_sem, near_sem, row_sem, t_sem, t_row_sem, edge_sem, yz_sem, gx_sem,
):
    g = lax.axis_index("gx")
    z = lax.axis_index("yz")
    barrier = pltpu.get_barrier_semaphore()
    for k in range(1, owners):
        pl.semaphore_signal(barrier, inc=1, device_id={"yz": lax.rem(z + k, owners)}, device_id_type=MESH)
    for k in range(1, slabs):
        pl.semaphore_signal(barrier, inc=1, device_id={"gx": lax.rem(g + k, slabs)}, device_id_type=MESH)

    table_copies = [
        pltpu.make_async_copy(fwd_hbm, fwd, table_sem.at[0]),
        pltpu.make_async_copy(inv_hbm, inv, table_sem.at[1]),
    ]
    for copy in table_copies:
        copy.start()

    has_low, has_high = z > 0, z < owners - 1
    has_prev, has_next = g > 0, g < slabs - 1

    def remote(src, dst, sems, device):
        return pltpu.make_async_remote_copy(
            src_ref=src, dst_ref=dst, send_sem=sems.at[0], recv_sem=sems.at[1],
            device_id=device, device_id_type=MESH,
        )

    def plane_copies(src, near, sems):
        up = remote(src, near.at[0], sems.at[0], {"yz": jnp.minimum(z + 1, owners - 1)})
        down = remote(src, near.at[1], sems.at[1], {"yz": jnp.maximum(z - 1, 0)})
        return up, down

    def row_copies(buf, sems):
        after = remote(
            buf.at[pl.ds(rows, PAD)], buf.at[pl.ds(0, PAD)], sems.at[0],
            {"gx": jnp.minimum(g + 1, slabs - 1)},
        )
        before = remote(
            buf.at[pl.ds(PAD, PAD)], buf.at[pl.ds(PAD + rows, PAD)], sems.at[1],
            {"gx": jnp.maximum(g - 1, 0)},
        )
        return after, before

    def start_pair(pair, to_first, to_second):
        @pl.when(to_first)
        def _():
            pair[0].start()

        @pl.when(to_second)
        def _():
            pair[1].start()

    def wait_pair(pair, has_before, has_after):
        @pl.when(has_after)
        def _():
            pair[0].wait_send()
            pair[1].wait_recv()

        @pl.when(has_before)
        def _():
            pair[1].wait_send()
            pair[0].wait_recv()

    def clear_rows(buf):
        @pl.when(jnp.logical_not(has_prev))
        def _():
            buf[pl.ds(0, PAD)] = jnp.zeros((PAD, NY), jnp.float32)

        @pl.when(jnp.logical_not(has_next))
        def _():
            buf[pl.ds(PAD + rows, PAD)] = jnp.zeros((PAD, NY), jnp.float32)

    def clear_planes(near):
        @pl.when(jnp.logical_not(has_low))
        def _():
            near[0] = jnp.zeros((rows, NY), jnp.float32)

        @pl.when(jnp.logical_not(has_high))
        def _():
            near[1] = jnp.zeros((rows, NY), jnp.float32)

    def place(b, carry):
        slot = anchor_ref[b]
        keep = fluid_ref[b]
        r0 = pl.multiple_of((b // y_bricks) * BR, BR)
        c0 = pl.multiple_of((b % y_bricks) * B, B)
        at = (pl.ds(r0, BR), pl.ds(c0, B))
        at_pad = (pl.ds(pl.multiple_of(r0 + PAD, PAD), BR), pl.ds(c0, B))
        root[at_pad] = jnp.sqrt(bricks_ref[slot, 0] * keep)
        accel_z[at] = bricks_ref[slot, 1] * keep
        accel_x[at_pad] = bricks_ref[slot, 2] * keep
        accel_y[at] = bricks_ref[slot, 3] * keep
        fluid[at] = jnp.full((BR, B), keep, jnp.float32)
        return carry

    lax.fori_loop(0, rows // BR * y_bricks, place, 0)

    pl.semaphore_wait(barrier, owners + slabs - 2)
    root_rows = root.at[pl.ds(PAD, rows)]
    near_pairs = [
        plane_copies(root_rows, near_root, near_sem.at[0]),
        plane_copies(accel_z, near_accel, near_sem.at[1]),
    ]
    row_pairs = [row_copies(root, row_sem.at[0]), row_copies(accel_x, row_sem.at[1])]
    for pair in row_pairs:
        start_pair(pair, has_next, has_prev)
    for pair in near_pairs:
        start_pair(pair, has_high, has_low)
    for buf in (root, accel_x, t_pad.at[0], t_pad.at[1]):
        clear_rows(buf)
    for buf in (near_root, near_accel, near_t.at[0], near_t.at[1]):
        clear_planes(buf)
    for pair in row_pairs:
        wait_pair(pair, has_prev, has_next)
    for pair in near_pairs:
        wait_pair(pair, has_low, has_high)

    lane = lax.broadcasted_iota(jnp.int32, (CHUNK, NY), 1)

    def left(value):
        return jnp.where(lane == 0, 0.0, pltpu.roll(value, 1, 1))

    def right(value):
        return jnp.where(lane == NY - 1, 0.0, pltpu.roll(value, NY - 1, 1))

    def at_chunk(i):
        r0 = pl.multiple_of(i * CHUNK, CHUNK)
        return pl.ds(r0, CHUNK), pl.ds(r0, CHUNK + 2 * PAD)

    def shifts(wide):
        return (
            wide[PAD - 1 : PAD - 1 + CHUNK],
            wide[PAD : PAD + CHUNK],
            wide[PAD + 1 : PAD + 1 + CHUNK],
        )

    def store_residual(at, value):
        residual_ref[0, at, :] = value
        high, low = split(value)
        res_hl[0, at, :] = high
        res_hl[1, at, :] = low

    def prepare(i, carry):
        at, wide_at = at_chunk(i)
        s_wide = root[wide_at, :]
        s_up, s, s_down = shifts(s_wide)
        ax_wide = accel_x[wide_at, :]
        ax = ax_wide[PAD : PAD + CHUNK]
        px_up, _, px_down = shifts(s_wide * ax_wide)
        ay = accel_y[at, :]
        py = s * ay
        s_left, s_right = left(s), right(s)
        s_low, s_high = near_root[0, at, :], near_root[1, at, :]
        az = accel_z[at, :]
        total = px_up - px_down + ax * (s_up - s_down)
        total = total + left(py) - right(py) + ay * (s_left - s_right)
        total = total + s_low * near_accel[0, at, :] - s_high * near_accel[1, at, :] + az * (s_low - s_high)
        store_residual(at, 0.5 * s * total)
        ring = s_up + s_down + s_left + s_right + s_low + s_high
        diagonal[at, :] = s * (shift_rate * s + ring) + (1.0 - fluid[at, :])
        return carry

    chunks = rows // CHUNK
    lax.fori_loop(0, chunks, prepare, 0)
    for copy in table_copies:
        copy.wait()

    tiles = NY // TILE

    def three(left_hl, right_hl):
        lh, ll = left_hl
        rh, rl = right_hl
        return dot32(lh, rh) + dot32(lh, rl) + dot32(ll, rh)

    def tile_at(j):
        return pl.ds(pl.multiple_of(j * TILE, TILE), TILE)

    def precondition(it):
        def forward(j, carry):
            at = tile_at(j)
            lines = three((res_hl[0], res_hl[1]), (fwd[0, :, at], fwd[1, :, at]))
            modes = three((table_x[0], table_x[1]), split(lines)) * inverse_ref[:, at]
            spec[:, at] = modes
            edge[it, 0:1, at] = jnp.sum(modes * ends_ref[:, 0:1], axis=0, keepdims=True)
            edge[it, 1:2, at] = jnp.sum(modes * ends_ref[:, B : B + 1], axis=0, keepdims=True)
            return carry

        edge[it] = jnp.zeros((8, NY), jnp.float32)
        lax.fori_loop(0, tiles, forward, 0)
        copies = [
            remote(edge.at[it], gathered.at[it, g], edge_sem.at[it, k], {"gx": lax.rem(g + k, slabs)})
            for k in range(1, slabs)
        ]
        for copy in copies:
            copy.start()
        gathered[it, g] = edge[it]
        for copy in copies:
            copy.wait()
        sides = []
        for side in range(2):
            total = jnp.zeros((1, NY), jnp.float32)
            for j in range(slabs):
                for end in range(2):
                    n = 2 * j + end
                    total = total + couple_ref[g, side, n : n + 1, :] * gathered[it, j, end : end + 1, :]
            sides.append(total)
        edge_y = jnp.concatenate(sides, axis=0)
        part[0:2, :] = edge_y

        def back_x(j, carry):
            at = tile_at(j)
            fix = ends_ref[:, 0:1] * part[0:1, at] + ends_ref[:, B : B + 1] * part[1:2, at]
            modes = spec[:, at] + inverse_ref[:, at] * fix
            high, low = split(three((table_xt[0], table_xt[1]), split(modes)))
            x_hl[0, :, at] = high
            x_hl[1, :, at] = low
            return carry

        lax.fori_loop(0, tiles, back_x, 0)
        pairs = []
        for j in range(tiles):
            at = pl.ds(j * TILE, TILE)
            out = three((x_hl[0], x_hl[1]), (inv[0, :, at], inv[1, :, at])) * fluid[:, at]
            update[it, :, at] = out
            t_pad[it, pl.ds(PAD, rows), at] = out * root[pl.ds(PAD, rows), at]
            pair = plane_copies(
                t_pad.at[it, pl.ds(PAD, rows), at], near_t.at[it, :, :, at], t_sem.at[it, j]
            )
            start_pair(pair, has_high, has_low)
            pairs.append(pair)
        rim = row_copies(t_pad.at[it], t_row_sem.at[it])
        start_pair(rim, has_next, has_prev)
        wait_pair(rim, has_prev, has_next)
        for pair in pairs:
            wait_pair(pair, has_low, has_high)

    def operate(it):
        def one(i, carry):
            energy, curve = carry
            at, wide_at = at_chunk(i)
            t_up, t, t_down = shifts(t_pad[it, wide_at, :])
            _, s, _ = shifts(root[wide_at, :])
            near = t_up + t_down + left(t) + right(t) + near_t[it, 0, at, :] + near_t[it, 1, at, :]
            u = update[it, at, :]
            out = diagonal[at, :] * u - s * near
            image[it, at, :] = out
            return energy + u * residual_ref[0, at, :], curve + u * out

        zero = jnp.zeros((CHUNK, NY), jnp.float32)
        energy, curve = lax.fori_loop(0, chunks, one, (zero, zero))
        row = lax.broadcasted_iota(jnp.int32, (8, B), 0)
        block = jnp.where(row < 4, jnp.sum(energy), jnp.sum(curve))
        for buf, sems, axis, count, index in (
            (total_yz, yz_sem, "yz", owners, z),
            (total_gx, gx_sem, "gx", slabs, g),
        ):
            buf[it, index] = block
            copies = [
                remote(buf.at[it, index], buf.at[it, index], sems.at[it, k], {axis: lax.rem(index + k, count)})
                for k in range(1, count)
            ]
            for copy in copies:
                copy.start()
            for copy in copies:
                copy.wait()
            block = buf[it, 0]
            for k in range(1, count):
                block = block + buf[it, k]
        return block[0:1, 0:1], block[4:5, 0:1]

    precondition(0)
    energy_now, curvature = operate(0)
    step_now = energy_now / curvature

    def advance(i, carry):
        at, _ = at_chunk(i)
        store_residual(at, residual_ref[0, at, :] - step_now * image[0, at, :])
        return carry

    lax.fori_loop(0, chunks, advance, 0)
    precondition(1)
    energy_next, curvature = operate(1)
    beta = energy_next / energy_now
    step_next = energy_next / (curvature - beta * energy_next / step_now)

    def finish(i, carry):
        at, _ = at_chunk(i)
        first, second = update[0, at, :], update[1, at, :]
        solution_ref[0, at, :] = step_now * first + step_next * (second + beta * first)
        residual_ref[0, at, :] = residual_ref[0, at, :] - step_next * (
            image[1, at, :] + beta * image[0, at, :]
        )
        return carry

    lax.fori_loop(0, chunks, finish, 0)


def solve(anchor, fluid, bricks, slabs, owners, rows, y_bricks):
    tables = [jnp.asarray(t) for t in solver_tables(slabs, rows)]
    plane = (rows, NY)
    padded = (rows + 2 * PAD, NY)
    f32, bf16 = jnp.float32, jnp.bfloat16
    vmem = pl.BlockSpec(memory_space=pltpu.VMEM)
    smem = pl.BlockSpec(memory_space=pltpu.SMEM)
    hbm = pl.BlockSpec(memory_space=pl.ANY)
    dma = pltpu.SemaphoreType.DMA
    out = jax.ShapeDtypeStruct((1,) + plane, f32)
    return pl.pallas_call(
        functools.partial(solver_kernel, slabs, owners, rows, y_bricks),
        out_shape=(out, out),
        in_specs=[smem, smem, vmem, hbm, hbm] + [vmem] * 5,
        out_specs=(vmem, vmem),
        scratch_shapes=[
            pltpu.VMEM((2, NY, NY), bf16),
            pltpu.VMEM((2, NY, NY), bf16),
            pltpu.VMEM(padded, f32),
            pltpu.VMEM(padded, f32),
            pltpu.VMEM(plane, f32),
            pltpu.VMEM(plane, f32),
            pltpu.VMEM(plane, f32),
            pltpu.VMEM(plane, f32),
            pltpu.VMEM((2,) + plane, f32),
            pltpu.VMEM((2,) + plane, f32),
            pltpu.VMEM((ITERS, 2) + plane, f32),
            pltpu.VMEM((ITERS,) + padded, f32),
            pltpu.VMEM((2,) + plane, bf16),
            pltpu.VMEM(plane, f32),
            pltpu.VMEM((2,) + plane, bf16),
            pltpu.VMEM((ITERS,) + plane, f32),
            pltpu.VMEM((ITERS,) + plane, f32),
            pltpu.VMEM((ITERS, 8, NY), f32),
            pltpu.VMEM((ITERS, slabs, 8, NY), f32),
            pltpu.VMEM((8, NY), f32),
            pltpu.VMEM((ITERS, owners, 8, B), f32),
            pltpu.VMEM((ITERS, slabs, 8, B), f32),
            dma((2,)),
            dma((2, 2, 2)),
            dma((2, 2, 2)),
            dma((ITERS, NY // TILE, 2, 2)),
            dma((ITERS, 2, 2)),
            dma((ITERS, slabs, 2)),
            dma((ITERS, owners, 2)),
            dma((ITERS, slabs, 2)),
        ],
        compiler_params=pltpu.CompilerParams(
            collective_id=1, has_side_effects=True, vmem_limit_bytes=60 * 2**20
        ),
        name="pressure_solver",
    )(anchor, fluid, bricks, *tables)


def ranks_of(owners_of, owner_count):
    one_hot = (owners_of[..., None] == jnp.arange(owner_count, dtype=jnp.int32)).astype(jnp.int32)
    earlier = jnp.cumsum(one_hot, axis=-2) - one_hot
    return jnp.sum(earlier * one_hot, axis=-1)


def on_device(camera_accel, camera_weight, brick_slot, brick_solid):
    owner_count = lax.axis_size("yz")
    slabs = lax.axis_size("gx")
    slot_count = brick_slot.shape[1]
    per_owner = 3 * slot_count // (2 * owner_count)
    rows = NX // slabs
    y_bricks = NY // B
    me = lax.axis_index("yz")
    slots = jnp.arange(slot_count, dtype=jnp.int32)

    brick_ids = brick_slot[0]
    owners_of = brick_ids // slot_count
    target = owners_of * per_owner + ranks_of(owners_of, owner_count)
    positions = jnp.arange(owner_count * per_owner, dtype=jnp.int32)
    matches = target[None, :] == positions[:, None]
    source = jnp.sum(jnp.where(matches, slots[None, :], 0), axis=1)

    all_ids = lax.all_gather(brick_ids, "yz")
    mine = all_ids // slot_count == me
    earlier = jnp.cumsum(mine.astype(jnp.int32), axis=1) - mine.astype(jnp.int32)
    place_of = jnp.arange(owner_count, dtype=jnp.int32)[:, None] * per_owner + earlier
    wanted = me * slot_count + slots
    arrived = all_ids.reshape(-1)[None, :] == wanted[:, None]
    anchor = jnp.sum(jnp.where(arrived, place_of.reshape(-1)[None, :], 0), axis=1)

    bricks = exchange(source, camera_accel[0], camera_weight[0], owner_count, per_owner)
    bricks = bricks.reshape((owner_count * per_owner,) + bricks.shape[2:])
    fluid = (1 - brick_solid[0]).astype(jnp.float32)
    return solve(anchor, fluid, bricks, slabs, owner_count, rows, y_bricks)


def solution(mesh):
    return jax.shard_map(
        on_device,
        mesh=mesh,
        in_specs=(
            P("gx", "yz", None, None, None),
            P("gx", "yz", None, None),
            P("gx", "yz"),
            P("gx", "yz"),
        ),
        out_specs=(P("yz", "gx", None), P("yz", "gx", None)),
        check_vma=False,
    )
```

```python
import functools

import jax
import jax.numpy as jnp
import ml_dtypes
import numpy as np
from jax import lax
from jax.experimental import pallas as pl
from jax.experimental.pallas import tpu as pltpu
from jax.sharding import PartitionSpec as P

NX = 1024
NY = 1024
BR = 16
B = 128
ITERS = 2

shift_rate = 0.05
spectral_gain = 1.0
spectral_floor = 2.0

MESH = pl.DeviceIdType.MESH
PAD = 8
CHUNK = BR
TILE = 256


def cosine_table(length):
    rows = np.arange(length, dtype=np.int64)[:, None]
    cols = np.arange(length, dtype=np.int64)[None, :]
    phases = (rows * (2 * cols + 1)) % (4 * length)
    scale = np.sqrt(np.where(rows == 0, 1.0, 2.0) / length)
    return scale * np.cos(phases * (np.pi / (2.0 * length)))


def eigen_values(length):
    return 2.0 - 2.0 * np.cos(np.arange(length) * (np.pi / length))


def high_low(table):
    high = table.astype(np.float32).astype(ml_dtypes.bfloat16)
    low = (table - high.astype(np.float64)).astype(np.float32).astype(ml_dtypes.bfloat16)
    return np.stack([high, low])


def solver_tables(slabs, rows):
    table_y = cosine_table(NY)
    table_x = cosine_table(rows)
    inverse = 1.0 / (
        spectral_gain * (eigen_values(rows)[:, None] + eigen_values(NY)[None, :]) + spectral_floor
    )
    first, last = table_x[:, :1], table_x[:, -1:]
    same = np.sum(first * first * inverse, axis=0)
    cross = np.sum(first * last * inverse, axis=0)
    faces = slabs - 1
    couple = np.zeros((slabs, 2, 2 * slabs, NY))
    if faces:
        matrix = np.zeros((NY, faces, faces))
        for i in range(faces):
            matrix[:, i, i] = 1.0 / spectral_gain + 2.0 * same
            if i:
                matrix[:, i, i - 1] = matrix[:, i - 1, i] = -cross
        solved = np.linalg.inv(matrix)
        for slab in range(slabs):
            for side, face, sign in ((0, slab - 1, 1.0), (1, slab, -1.0)):
                if 0 <= face < faces:
                    for other in range(faces):
                        couple[slab, side, 2 * other + 1] += sign * solved[:, face, other]
                        couple[slab, side, 2 * other + 2] -= sign * solved[:, face, other]
    ends = np.concatenate([np.repeat(first, B, 1), np.repeat(last, B, 1)], axis=1)
    return (
        high_low(table_y.T),
        high_low(table_y),
        high_low(table_x),
        high_low(table_x.T),
        inverse.astype(np.float32),
        ends.astype(np.float32),
        couple.astype(np.float32),
    )


def exchange_kernel(
    owners, per_owner, src_ref, ids_ref, accel_ref, weight_ref, main_out, side_out,
    main, side, main_send, main_recv, side_send, side_recv,
):
    me = lax.axis_index("yz")
    barrier = pltpu.get_barrier_semaphore()
    for k in range(1, owners):
        pl.semaphore_signal(
            barrier, inc=1, device_id={"yz": lax.rem(me + k, owners)}, device_id_type=MESH
        )
    row_cells, col_cells = weight_ref.shape[1:]
    row = lax.broadcasted_iota(jnp.int32, (row_cells, col_cells), 0)
    lane = lax.broadcasted_iota(jnp.int32, (row_cells, col_cells), 1)
    held = side_rows(per_owner)

    def pack(k, owner):
        def one(p, cols):
            slot = src_ref[owner * per_owner + p]
            root = jnp.sqrt(weight_ref[slot])
            ax, ay = accel_ref[slot, 1], accel_ref[slot, 2]
            px, py = root * ax, root * ay
            s_up = jnp.where(row == 0, 0.0, pltpu.roll(root, 1, 0))
            s_down = jnp.where(row == row_cells - 1, 0.0, pltpu.roll(root, row_cells - 1, 0))
            s_left = jnp.where(lane == 0, 0.0, pltpu.roll(root, 1, 1))
            s_right = jnp.where(lane == col_cells - 1, 0.0, pltpu.roll(root, col_cells - 1, 1))
            p_up = jnp.where(row == 0, 0.0, pltpu.roll(px, 1, 0))
            p_down = jnp.where(row == row_cells - 1, 0.0, pltpu.roll(px, row_cells - 1, 0))
            p_left = jnp.where(lane == 0, 0.0, pltpu.roll(py, 1, 1))
            p_right = jnp.where(lane == col_cells - 1, 0.0, pltpu.roll(py, col_cells - 1, 1))
            total = p_up - p_down + p_left - p_right + ax * (s_up - s_down) + ay * (s_left - s_right)
            main[k, p, 0] = root
            main[k, p, 1] = accel_ref[slot, 0]
            main[k, p, 2] = 0.5 * root * total
            side[k, pl.ds(p, 1), :] = ax[0:1]
            side[k, pl.ds(held + p, 1), :] = ax[row_cells - 1 : row_cells]
            cols = jnp.where(lane == 2 * p, ay[:, 0:1], cols)
            return jnp.where(lane == 2 * p + 1, ay[:, col_cells - 1 : col_cells], cols)

        cols = lax.fori_loop(0, per_owner, one, jnp.zeros((row_cells, col_cells), jnp.float32))
        side[k, 2 * held : 2 * held + row_cells, :] = cols
        side[k, 2 * held + row_cells :, :] = ids_ref[owner]

    side[...] = jnp.zeros_like(side)
    copies = []
    for k in range(1, owners):
        owner = lax.rem(me + k, owners)
        pack(k, owner)
        if k == 1:
            pl.semaphore_wait(barrier, owners - 1)
        for src, dst, send, recv in (
            (main, main_out, main_send, main_recv),
            (side, side_out, side_send, side_recv),
        ):
            copy = pltpu.make_async_remote_copy(
                src_ref=src.at[k],
                dst_ref=dst.at[me],
                send_sem=send.at[k],
                recv_sem=recv.at[k],
                device_id={"yz": owner},
                device_id_type=MESH,
            )
            copy.start()
            copies.append(copy)
    pack(0, me)
    own = [
        pltpu.make_async_copy(main.at[0], main_out.at[me], main_send.at[0]),
        pltpu.make_async_copy(side.at[0], side_out.at[me], side_send.at[0]),
    ]
    for copy in own:
        copy.start()
    for copy in own:
        copy.wait()
    for copy in copies:
        copy.wait()


def side_rows(per_owner):
    return -(-per_owner // 8) * 8


def exchange(source, ids, accel, weight, owners, per_owner):
    slots, _, row_cells, col_cells = accel.shape
    main_shape = (owners, per_owner, 3, row_cells, col_cells)
    side_shape = (owners, 2 * side_rows(per_owner) + row_cells + 8, col_cells)
    return pl.pallas_call(
        functools.partial(exchange_kernel, owners, per_owner),
        out_shape=(
            jax.ShapeDtypeStruct(main_shape, jnp.float32),
            jax.ShapeDtypeStruct(side_shape, jnp.float32),
        ),
        in_specs=[pl.BlockSpec(memory_space=pltpu.SMEM)] + [pl.BlockSpec(memory_space=pltpu.VMEM)] * 3,
        out_specs=(pl.BlockSpec(memory_space=pl.ANY), pl.BlockSpec(memory_space=pl.ANY)),
        scratch_shapes=[
            pltpu.VMEM(main_shape, jnp.float32),
            pltpu.VMEM(side_shape, jnp.float32),
        ]
        + [pltpu.SemaphoreType.DMA((owners,))] * 4,
        compiler_params=pltpu.CompilerParams(
            collective_id=0, has_side_effects=True, vmem_limit_bytes=40 * 2**20
        ),
        name="brick_exchange",
    )(source, ids, accel, weight)


def split(value):
    high = value.astype(jnp.bfloat16)
    return high, (value - high.astype(jnp.float32)).astype(jnp.bfloat16)


def dot32(left, right):
    return jnp.dot(left, right, preferred_element_type=jnp.float32)


def solver_kernel(
    slabs, owners, rows, y_bricks, per_owner,
    from_ref, place_ref, fluid_ref, main_ref, side_ref, fwd_hbm, inv_hbm, table_x, table_xt, inverse_ref, ends_ref, couple_ref,
    solution_ref, residual_ref,
    fwd, inv, root, accel_x, accel_y, accel_z, source, fluid, diagonal, near_root, near_accel, near_t, t_pad,
    res_hl, spec, x_hl, update, image, edge, gathered, part, total_yz, total_gx,
    table_sem, near_sem, row_sem, t_sem, t_row_sem, edge_sem, yz_sem, gx_sem,
):
    g = lax.axis_index("gx")
    z = lax.axis_index("yz")
    barrier = pltpu.get_barrier_semaphore()
    for k in range(1, owners):
        pl.semaphore_signal(barrier, inc=1, device_id={"yz": lax.rem(z + k, owners)}, device_id_type=MESH)
    for k in range(1, slabs):
        pl.semaphore_signal(barrier, inc=1, device_id={"gx": lax.rem(g + k, slabs)}, device_id_type=MESH)

    table_copies = [
        pltpu.make_async_copy(fwd_hbm, fwd, table_sem.at[0]),
        pltpu.make_async_copy(inv_hbm, inv, table_sem.at[1]),
    ]
    for copy in table_copies:
        copy.start()

    has_low, has_high = z > 0, z < owners - 1
    has_prev, has_next = g > 0, g < slabs - 1

    def remote(src, dst, sems, device):
        return pltpu.make_async_remote_copy(
            src_ref=src, dst_ref=dst, send_sem=sems.at[0], recv_sem=sems.at[1],
            device_id=device, device_id_type=MESH,
        )

    def plane_copies(src, near, sems):
        up = remote(src, near.at[0], sems.at[0], {"yz": jnp.minimum(z + 1, owners - 1)})
        down = remote(src, near.at[1], sems.at[1], {"yz": jnp.maximum(z - 1, 0)})
        return up, down

    def row_copies(buf, sems):
        after = remote(
            buf.at[pl.ds(rows, PAD)], buf.at[pl.ds(0, PAD)], sems.at[0],
            {"gx": jnp.minimum(g + 1, slabs - 1)},
        )
        before = remote(
            buf.at[pl.ds(PAD, PAD)], buf.at[pl.ds(PAD + rows, PAD)], sems.at[1],
            {"gx": jnp.maximum(g - 1, 0)},
        )
        return after, before

    def start_pair(pair, to_first, to_second):
        @pl.when(to_first)
        def _():
            pair[0].start()

        @pl.when(to_second)
        def _():
            pair[1].start()

    def wait_pair(pair, has_before, has_after):
        @pl.when(has_after)
        def _():
            pair[0].wait_send()
            pair[1].wait_recv()

        @pl.when(has_before)
        def _():
            pair[1].wait_send()
            pair[0].wait_recv()

    def clear_rows(buf):
        @pl.when(jnp.logical_not(has_prev))
        def _():
            buf[pl.ds(0, PAD)] = jnp.zeros((PAD, NY), jnp.float32)

        @pl.when(jnp.logical_not(has_next))
        def _():
            buf[pl.ds(PAD + rows, PAD)] = jnp.zeros((PAD, NY), jnp.float32)

    def clear_planes(near):
        @pl.when(jnp.logical_not(has_low))
        def _():
            near[0] = jnp.zeros((rows, NY), jnp.float32)

        @pl.when(jnp.logical_not(has_high))
        def _():
            near[1] = jnp.zeros((rows, NY), jnp.float32)

    held = side_rows(per_owner)
    brick_row = lax.broadcasted_iota(jnp.int32, (BR, B), 0)
    brick_lane = lax.broadcasted_iota(jnp.int32, (BR, B), 1)

    def place(b, carry):
        owner = from_ref[b]
        p = place_ref[b]
        keep = fluid_ref[b]
        r0 = pl.multiple_of((b // y_bricks) * BR, BR)
        c0 = pl.multiple_of((b % y_bricks) * B, B)
        at = (pl.ds(r0, BR), pl.ds(c0, B))
        at_pad = (pl.ds(pl.multiple_of(r0 + PAD, PAD), BR), pl.ds(c0, B))
        root[at_pad] = main_ref[owner, p, 0] * keep
        accel_z[at] = main_ref[owner, p, 1] * keep
        source[at] = main_ref[owner, p, 2] * keep
        top = side_ref[owner, pl.ds(p, 1), :]
        bottom = side_ref[owner, pl.ds(held + p, 1), :]
        cols = side_ref[owner, 2 * held : 2 * held + BR, :]
        begin = jnp.sum(jnp.where(brick_lane == 2 * p, cols, 0.0), axis=1, keepdims=True)
        end = jnp.sum(jnp.where(brick_lane == 2 * p + 1, cols, 0.0), axis=1, keepdims=True)
        accel_x[at_pad] = keep * jnp.where(
            brick_row == 0, top, jnp.where(brick_row == BR - 1, bottom, 0.0)
        )
        accel_y[at] = keep * jnp.where(
            brick_lane == 0, begin, jnp.where(brick_lane == B - 1, end, 0.0)
        )
        fluid[at] = jnp.full((BR, B), keep, jnp.float32)
        return carry

    lax.fori_loop(0, rows // BR * y_bricks, place, 0, unroll=2)

    pl.semaphore_wait(barrier, owners + slabs - 2)
    root_rows = root.at[pl.ds(PAD, rows)]
    near_pairs = [
        plane_copies(root_rows, near_root, near_sem.at[0]),
        plane_copies(accel_z, near_accel, near_sem.at[1]),
    ]
    row_pairs = [row_copies(root, row_sem.at[0]), row_copies(accel_x, row_sem.at[1])]
    for pair in row_pairs:
        start_pair(pair, has_next, has_prev)
    for pair in near_pairs:
        start_pair(pair, has_high, has_low)
    for buf in (root, accel_x, t_pad.at[0], t_pad.at[1]):
        clear_rows(buf)
    for buf in (near_root, near_accel, near_t.at[0], near_t.at[1]):
        clear_planes(buf)
    for pair in row_pairs:
        wait_pair(pair, has_prev, has_next)
    for pair in near_pairs:
        wait_pair(pair, has_low, has_high)

    row = lax.broadcasted_iota(jnp.int32, (CHUNK, NY), 0)
    lane = lax.broadcasted_iota(jnp.int32, (CHUNK, NY), 1)

    def left(value):
        return jnp.where(lane == 0, 0.0, pltpu.roll(value, 1, 1))

    def right(value):
        return jnp.where(lane == NY - 1, 0.0, pltpu.roll(value, NY - 1, 1))

    def at_chunk(i):
        r0 = pl.multiple_of(i * CHUNK, CHUNK)
        return pl.ds(r0, CHUNK), pl.ds(r0, CHUNK + 2 * PAD)

    def shifts(wide):
        return (
            wide[PAD - 1 : PAD - 1 + CHUNK],
            wide[PAD : PAD + CHUNK],
            wide[PAD + 1 : PAD + 1 + CHUNK],
        )

    def store_residual(at, value):
        residual_ref[0, at, :] = value
        high, low = split(value)
        res_hl[0, at, :] = high
        res_hl[1, at, :] = low

    def prepare(i, carry):
        at, wide_at = at_chunk(i)
        s_wide = root[wide_at, :]
        s_up, s, s_down = shifts(s_wide)
        ax_wide = accel_x[wide_at, :]
        ax = ax_wide[PAD : PAD + CHUNK]
        px_up, _, px_down = shifts(s_wide * ax_wide)
        ay = accel_y[at, :]
        py = s * ay
        s_left, s_right = left(s), right(s)
        s_low, s_high = near_root[0, at, :], near_root[1, at, :]
        az = accel_z[at, :]
        total = jnp.where(row == 0, px_up + ax * s_up, 0.0)
        total = total - jnp.where(row == CHUNK - 1, px_down + ax * s_down, 0.0)
        total = total + jnp.where(lane % B == 0, left(py) + ay * s_left, 0.0)
        total = total - jnp.where(lane % B == B - 1, right(py) + ay * s_right, 0.0)
        total = total + s_low * near_accel[0, at, :] - s_high * near_accel[1, at, :] + az * (s_low - s_high)
        store_residual(at, source[at, :] + 0.5 * s * total)
        ring = s_up + s_down + s_left + s_right + s_low + s_high
        diagonal[at, :] = s * (shift_rate * s + ring) + (1.0 - fluid[at, :])
        return carry

    chunks = rows // CHUNK
    lax.fori_loop(0, chunks, prepare, 0)
    for copy in table_copies:
        copy.wait()

    tiles = NY // TILE

    def three(left_hl, right_hl):
        lh, ll = left_hl
        rh, rl = right_hl
        return dot32(lh, rh) + dot32(lh, rl) + dot32(ll, rh)

    def tile_at(j):
        return pl.ds(pl.multiple_of(j * TILE, TILE), TILE)

    def precondition(it):
        def forward(j, carry):
            at = tile_at(j)
            lines = three((res_hl[0], res_hl[1]), (fwd[0, :, at], fwd[1, :, at]))
            modes = three((table_x[0], table_x[1]), split(lines)) * inverse_ref[:, at]
            spec[:, at] = modes
            edge[it, 0:1, at] = jnp.sum(modes * ends_ref[:, 0:1], axis=0, keepdims=True)
            edge[it, 1:2, at] = jnp.sum(modes * ends_ref[:, B : B + 1], axis=0, keepdims=True)
            return carry

        edge[it] = jnp.zeros((8, NY), jnp.float32)
        lax.fori_loop(0, tiles, forward, 0)
        copies = [
            remote(edge.at[it], gathered.at[it, g], edge_sem.at[it, k], {"gx": lax.rem(g + k, slabs)})
            for k in range(1, slabs)
        ]
        for copy in copies:
            copy.start()
        gathered[it, g] = edge[it]
        for copy in copies:
            copy.wait()
        sides = []
        for side in range(2):
            total = jnp.zeros((1, NY), jnp.float32)
            for j in range(slabs):
                for end in range(2):
                    n = 2 * j + end
                    total = total + couple_ref[g, side, n : n + 1, :] * gathered[it, j, end : end + 1, :]
            sides.append(total)
        edge_y = jnp.concatenate(sides, axis=0)
        part[0:2, :] = edge_y

        def back_x(j, carry):
            at = tile_at(j)
            fix = ends_ref[:, 0:1] * part[0:1, at] + ends_ref[:, B : B + 1] * part[1:2, at]
            modes = spec[:, at] + inverse_ref[:, at] * fix
            high, low = split(three((table_xt[0], table_xt[1]), split(modes)))
            x_hl[0, :, at] = high
            x_hl[1, :, at] = low
            return carry

        lax.fori_loop(0, tiles, back_x, 0)
        pairs = []
        for j in range(tiles):
            at = pl.ds(j * TILE, TILE)
            out = three((x_hl[0], x_hl[1]), (inv[0, :, at], inv[1, :, at])) * fluid[:, at]
            update[it, :, at] = out
            t_pad[it, pl.ds(PAD, rows), at] = out * root[pl.ds(PAD, rows), at]
            pair = plane_copies(
                t_pad.at[it, pl.ds(PAD, rows), at], near_t.at[it, :, :, at], t_sem.at[it, j]
            )
            start_pair(pair, has_high, has_low)
            pairs.append(pair)
        rim = row_copies(t_pad.at[it], t_row_sem.at[it])
        start_pair(rim, has_next, has_prev)
        wait_pair(rim, has_prev, has_next)
        for pair in pairs:
            wait_pair(pair, has_low, has_high)

    def operate(it):
        def one(i, carry):
            energy, curve = carry
            at, wide_at = at_chunk(i)
            t_up, t, t_down = shifts(t_pad[it, wide_at, :])
            _, s, _ = shifts(root[wide_at, :])
            near = t_up + t_down + left(t) + right(t) + near_t[it, 0, at, :] + near_t[it, 1, at, :]
            u = update[it, at, :]
            out = diagonal[at, :] * u - s * near
            image[it, at, :] = out
            return energy + u * residual_ref[0, at, :], curve + u * out

        zero = jnp.zeros((CHUNK, NY), jnp.float32)
        energy, curve = lax.fori_loop(0, chunks, one, (zero, zero))
        half = lax.broadcasted_iota(jnp.int32, (8, B), 0)
        block = jnp.where(half < 4, jnp.sum(energy), jnp.sum(curve))
        for buf, sems, axis, count, index in (
            (total_yz, yz_sem, "yz", owners, z),
            (total_gx, gx_sem, "gx", slabs, g),
        ):
            buf[it, index] = block
            copies = [
                remote(buf.at[it, index], buf.at[it, index], sems.at[it, k], {axis: lax.rem(index + k, count)})
                for k in range(1, count)
            ]
            for copy in copies:
                copy.start()
            for copy in copies:
                copy.wait()
            block = buf[it, 0]
            for k in range(1, count):
                block = block + buf[it, k]
        return block[0:1, 0:1], block[4:5, 0:1]

    precondition(0)
    energy_now, curvature = operate(0)
    step_now = energy_now / curvature

    def advance(i, carry):
        at, _ = at_chunk(i)
        store_residual(at, residual_ref[0, at, :] - step_now * image[0, at, :])
        return carry

    lax.fori_loop(0, chunks, advance, 0)
    precondition(1)
    energy_next, curvature = operate(1)
    beta = energy_next / energy_now
    step_next = energy_next / (curvature - beta * energy_next / step_now)

    def finish(i, carry):
        at, _ = at_chunk(i)
        first, second = update[0, at, :], update[1, at, :]
        solution_ref[0, at, :] = step_now * first + step_next * (second + beta * first)
        residual_ref[0, at, :] = residual_ref[0, at, :] - step_next * (
            image[1, at, :] + beta * image[0, at, :]
        )
        return carry

    lax.fori_loop(0, chunks, finish, 0)


def solve(owner_of, place_of, fluid, main, side, slabs, owners, rows, y_bricks):
    tables = [jnp.asarray(t) for t in solver_tables(slabs, rows)]
    plane = (rows, NY)
    padded = (rows + 2 * PAD, NY)
    f32, bf16 = jnp.float32, jnp.bfloat16
    vmem = pl.BlockSpec(memory_space=pltpu.VMEM)
    smem = pl.BlockSpec(memory_space=pltpu.SMEM)
    hbm = pl.BlockSpec(memory_space=pl.ANY)
    dma = pltpu.SemaphoreType.DMA
    out = jax.ShapeDtypeStruct((1,) + plane, f32)
    return pl.pallas_call(
        functools.partial(solver_kernel, slabs, owners, rows, y_bricks, main.shape[1]),
        out_shape=(out, out),
        in_specs=[smem] * 3 + [vmem, vmem, hbm, hbm] + [vmem] * 5,
        out_specs=(vmem, vmem),
        scratch_shapes=[
            pltpu.VMEM((2, NY, NY), bf16),
            pltpu.VMEM((2, NY, NY), bf16),
            pltpu.VMEM(padded, f32),
            pltpu.VMEM(padded, f32),
            pltpu.VMEM(plane, f32),
            pltpu.VMEM(plane, f32),
            pltpu.VMEM(plane, f32),
            pltpu.VMEM(plane, f32),
            pltpu.VMEM(plane, f32),
            pltpu.VMEM((2,) + plane, f32),
            pltpu.VMEM((2,) + plane, f32),
            pltpu.VMEM((ITERS, 2) + plane, f32),
            pltpu.VMEM((ITERS,) + padded, f32),
            pltpu.VMEM((2,) + plane, bf16),
            pltpu.VMEM(plane, f32),
            pltpu.VMEM((2,) + plane, bf16),
            pltpu.VMEM((ITERS,) + plane, f32),
            pltpu.VMEM((ITERS,) + plane, f32),
            pltpu.VMEM((ITERS, 8, NY), f32),
            pltpu.VMEM((ITERS, slabs, 8, NY), f32),
            pltpu.VMEM((8, NY), f32),
            pltpu.VMEM((ITERS, owners, 8, B), f32),
            pltpu.VMEM((ITERS, slabs, 8, B), f32),
            dma((2,)),
            dma((2, 2, 2)),
            dma((2, 2, 2)),
            dma((ITERS, NY // TILE, 2, 2)),
            dma((ITERS, 2, 2)),
            dma((ITERS, slabs, 2)),
            dma((ITERS, owners, 2)),
            dma((ITERS, slabs, 2)),
        ],
        compiler_params=pltpu.CompilerParams(
            collective_id=1, has_side_effects=True, vmem_limit_bytes=60 * 2**20
        ),
        name="pressure_solver",
    )(owner_of, place_of, fluid, main, side, *tables)


def ranks_of(owners_of, owner_count):
    one_hot = (owners_of[..., None] == jnp.arange(owner_count, dtype=jnp.int32)).astype(jnp.int32)
    earlier = jnp.cumsum(one_hot, axis=-2) - one_hot
    return jnp.sum(earlier * one_hot, axis=-1)


def on_device(camera_accel, camera_weight, brick_slot, brick_solid):
    owner_count = lax.axis_size("yz")
    slabs = lax.axis_size("gx")
    slot_count = brick_slot.shape[1]
    per_owner = 3 * slot_count // (2 * owner_count)
    rows = NX // slabs
    y_bricks = NY // B
    slots = jnp.arange(slot_count, dtype=jnp.int32)

    brick_ids = brick_slot[0]
    owners_of = brick_ids // slot_count
    target = owners_of * per_owner + ranks_of(owners_of, owner_count)
    positions = jnp.arange(owner_count * per_owner, dtype=jnp.int32)
    matches = target[None, :] == positions[:, None]
    source = jnp.sum(jnp.where(matches, slots[None, :], 0), axis=1)

    found = jnp.sum(jnp.where(matches, 1 + brick_ids[None, :] % slot_count, 0), axis=1) - 1
    ids = jnp.pad(
        found.astype(jnp.float32).reshape(owner_count, 1, per_owner),
        ((0, 0), (0, 7), (0, B - per_owner)),
        constant_values=-1.0,
    )
    main, side = exchange(source, ids, camera_accel[0], camera_weight[0], owner_count, per_owner)
    held_ids = side[:, -8, :per_owner].reshape(-1)
    arrived = held_ids[None, :] == slots.astype(jnp.float32)[:, None]
    anchor = jnp.sum(jnp.where(arrived, positions[None, :], 0), axis=1)
    fluid = (1 - brick_solid[0]).astype(jnp.float32)
    return solve(
        anchor // per_owner, anchor % per_owner, fluid, main, side, slabs, owner_count, rows, y_bricks
    )


def solution(mesh):
    return jax.shard_map(
        on_device,
        mesh=mesh,
        in_specs=(
            P("gx", "yz", None, None, None),
            P("gx", "yz", None, None),
            P("gx", "yz"),
            P("gx", "yz"),
        ),
        out_specs=(P("yz", "gx", None), P("yz", "gx", None)),
        check_vma=False,
    )
```

```python
import functools

import jax
import jax.numpy as jnp
import ml_dtypes
import numpy as np
from jax import lax
from jax.experimental import pallas as pl
from jax.experimental.pallas import tpu as pltpu
from jax.sharding import PartitionSpec as P

NX = 1024
NY = 1024
BR = 16
B = 128
ITERS = 2

shift_rate = 0.05
spectral_gain = 1.0
spectral_floor = 2.0

MESH = pl.DeviceIdType.MESH
PAD = 8
CHUNK = BR
TILE = 256


def cosine_table(length):
    rows = np.arange(length, dtype=np.int64)[:, None]
    cols = np.arange(length, dtype=np.int64)[None, :]
    phases = (rows * (2 * cols + 1)) % (4 * length)
    scale = np.sqrt(np.where(rows == 0, 1.0, 2.0) / length)
    return scale * np.cos(phases * (np.pi / (2.0 * length)))


def eigen_values(length):
    return 2.0 - 2.0 * np.cos(np.arange(length) * (np.pi / length))


def high_low(table):
    high = table.astype(np.float32).astype(ml_dtypes.bfloat16)
    low = (table - high.astype(np.float64)).astype(np.float32).astype(ml_dtypes.bfloat16)
    return np.stack([high, low])


def solver_tables(slabs, rows):
    table_y = cosine_table(NY)
    table_x = cosine_table(rows)
    inverse = 1.0 / (
        spectral_gain * (eigen_values(rows)[:, None] + eigen_values(NY)[None, :]) + spectral_floor
    )
    first, last = table_x[:, :1], table_x[:, -1:]
    same = np.sum(first * first * inverse, axis=0)
    cross = np.sum(first * last * inverse, axis=0)
    faces = slabs - 1
    couple = np.zeros((slabs, 2, 2 * slabs, NY))
    if faces:
        matrix = np.zeros((NY, faces, faces))
        for i in range(faces):
            matrix[:, i, i] = 1.0 / spectral_gain + 2.0 * same
            if i:
                matrix[:, i, i - 1] = matrix[:, i - 1, i] = -cross
        solved = np.linalg.inv(matrix)
        for slab in range(slabs):
            for side, face, sign in ((0, slab - 1, 1.0), (1, slab, -1.0)):
                if 0 <= face < faces:
                    for other in range(faces):
                        couple[slab, side, 2 * other + 1] += sign * solved[:, face, other]
                        couple[slab, side, 2 * other + 2] -= sign * solved[:, face, other]
    ends = np.concatenate([np.repeat(first, B, 1), np.repeat(last, B, 1)], axis=1)
    return (
        high_low(table_y.T),
        high_low(table_y),
        high_low(table_x),
        high_low(table_x.T),
        inverse.astype(np.float32),
        ends.astype(np.float32),
        couple.astype(np.float32),
    )


def exchange_kernel(
    owners, per_owner, src_ref, ids_ref, accel_ref, weight_ref, main_out, side_out,
    main, side, main_send, main_recv, side_send, side_recv,
):
    me = lax.axis_index("yz")
    barrier = pltpu.get_barrier_semaphore()
    for k in range(1, owners):
        pl.semaphore_signal(
            barrier, inc=1, device_id={"yz": lax.rem(me + k, owners)}, device_id_type=MESH
        )
    row_cells, col_cells = weight_ref.shape[1:]
    row = lax.broadcasted_iota(jnp.int32, (row_cells, col_cells), 0)
    lane = lax.broadcasted_iota(jnp.int32, (row_cells, col_cells), 1)
    held = side_rows(per_owner)

    def pack(k, owner):
        def one(p, cols):
            slot = src_ref[owner * per_owner + p]
            root = jnp.sqrt(weight_ref[slot])
            ax, ay = accel_ref[slot, 1], accel_ref[slot, 2]
            px, py = root * ax, root * ay
            s_up = jnp.where(row == 0, 0.0, pltpu.roll(root, 1, 0))
            s_down = jnp.where(row == row_cells - 1, 0.0, pltpu.roll(root, row_cells - 1, 0))
            s_left = jnp.where(lane == 0, 0.0, pltpu.roll(root, 1, 1))
            s_right = jnp.where(lane == col_cells - 1, 0.0, pltpu.roll(root, col_cells - 1, 1))
            p_up = jnp.where(row == 0, 0.0, pltpu.roll(px, 1, 0))
            p_down = jnp.where(row == row_cells - 1, 0.0, pltpu.roll(px, row_cells - 1, 0))
            p_left = jnp.where(lane == 0, 0.0, pltpu.roll(py, 1, 1))
            p_right = jnp.where(lane == col_cells - 1, 0.0, pltpu.roll(py, col_cells - 1, 1))
            total = p_up - p_down + p_left - p_right + ax * (s_up - s_down) + ay * (s_left - s_right)
            main[k, p, 0] = root
            main[k, p, 1] = accel_ref[slot, 0]
            main[k, p, 2] = 0.5 * root * total
            side[k, pl.ds(p, 1), :] = ax[0:1]
            side[k, pl.ds(held + p, 1), :] = ax[row_cells - 1 : row_cells]
            cols = jnp.where(lane == 2 * p, ay[:, 0:1], cols)
            return jnp.where(lane == 2 * p + 1, ay[:, col_cells - 1 : col_cells], cols)

        cols = lax.fori_loop(0, per_owner, one, jnp.zeros((row_cells, col_cells), jnp.float32))
        side[k, 2 * held : 2 * held + row_cells, :] = cols
        side[k, 2 * held + row_cells :, :] = ids_ref[owner]

    side[...] = jnp.zeros_like(side)
    copies = []
    for k in range(1, owners):
        owner = lax.rem(me + k, owners)
        pack(k, owner)
        if k == 1:
            pl.semaphore_wait(barrier, owners - 1)
        for src, dst, send, recv in (
            (main, main_out, main_send, main_recv),
            (side, side_out, side_send, side_recv),
        ):
            copy = pltpu.make_async_remote_copy(
                src_ref=src.at[k],
                dst_ref=dst.at[me],
                send_sem=send.at[k],
                recv_sem=recv.at[k],
                device_id={"yz": owner},
                device_id_type=MESH,
            )
            copy.start()
            copies.append(copy)
    pack(0, me)
    own = [
        pltpu.make_async_copy(main.at[0], main_out.at[me], main_send.at[0]),
        pltpu.make_async_copy(side.at[0], side_out.at[me], side_send.at[0]),
    ]
    for copy in own:
        copy.start()
    for copy in own:
        copy.wait()
    for copy in copies:
        copy.wait()


def side_rows(per_owner):
    return -(-per_owner // 8) * 8


def exchange(source, ids, accel, weight, owners, per_owner):
    slots, _, row_cells, col_cells = accel.shape
    main_shape = (owners, per_owner, 3, row_cells, col_cells)
    side_shape = (owners, 2 * side_rows(per_owner) + row_cells + 8, col_cells)
    return pl.pallas_call(
        functools.partial(exchange_kernel, owners, per_owner),
        out_shape=(
            jax.ShapeDtypeStruct(main_shape, jnp.float32),
            jax.ShapeDtypeStruct(side_shape, jnp.float32),
        ),
        in_specs=[pl.BlockSpec(memory_space=pltpu.SMEM)] + [pl.BlockSpec(memory_space=pltpu.VMEM)] * 3,
        out_specs=(pl.BlockSpec(memory_space=pl.ANY), pl.BlockSpec(memory_space=pl.ANY)),
        scratch_shapes=[
            pltpu.VMEM(main_shape, jnp.float32),
            pltpu.VMEM(side_shape, jnp.float32),
        ]
        + [pltpu.SemaphoreType.DMA((owners,))] * 4,
        compiler_params=pltpu.CompilerParams(
            collective_id=0, has_side_effects=True, vmem_limit_bytes=40 * 2**20
        ),
        name="brick_exchange",
    )(source, ids, accel, weight)


def split(value):
    high = value.astype(jnp.bfloat16)
    return high, (value - high.astype(jnp.float32)).astype(jnp.bfloat16)


def dot32(left, right):
    return jnp.dot(left, right, preferred_element_type=jnp.float32)


def solver_kernel(
    slabs, owners, rows, y_bricks, per_owner,
    from_ref, place_ref, fluid_ref, main_ref, side_ref, fwd_hbm, inv_hbm, table_x, table_xt, inverse_ref, ends_ref, couple_ref,
    solution_ref, residual_ref,
    fwd, inv, root, accel_x, accel_y, accel_z, source, fluid, diagonal, near_root, near_accel, near_t, t_pad,
    res_hl, spec, x_hl, update, image, edge, gathered, part, total_yz, total_gx, relay,
    table_sem, near_sem, row_sem, t_sem, t_row_sem, edge_sem, yz_sem, gx_sem,
):
    g = lax.axis_index("gx")
    z = lax.axis_index("yz")
    barrier = pltpu.get_barrier_semaphore()
    for k in range(1, owners):
        pl.semaphore_signal(barrier, inc=1, device_id={"yz": lax.rem(z + k, owners)}, device_id_type=MESH)
    for k in range(1, slabs):
        pl.semaphore_signal(barrier, inc=1, device_id={"gx": lax.rem(g + k, slabs)}, device_id_type=MESH)

    table_copies = [
        pltpu.make_async_copy(fwd_hbm, fwd, table_sem.at[0]),
        pltpu.make_async_copy(inv_hbm, inv, table_sem.at[1]),
    ]
    for copy in table_copies:
        copy.start()

    has_low, has_high = z > 0, z < owners - 1
    has_prev, has_next = g > 0, g < slabs - 1

    def remote(src, dst, sems, device):
        return pltpu.make_async_remote_copy(
            src_ref=src, dst_ref=dst, send_sem=sems.at[0], recv_sem=sems.at[1],
            device_id=device, device_id_type=MESH,
        )

    half = rows // 2
    middle = owners // 2
    via = (0, owners - 1)
    tiles = NY // TILE

    class Piece:
        def __init__(self, src, near, held, sems):
            parts = [pl.ds(0, half), pl.ds(half, half)]

            def copy(src, dst, send, recv, device):
                return pltpu.make_async_remote_copy(
                    src_ref=src, dst_ref=dst, send_sem=sems.at[send], recv_sem=sems.at[recv],
                    device_id={"yz": device}, device_id_type=MESH,
                )

            self.up = copy(src, near.at[0], 0, 1, jnp.minimum(z + 1, owners - 1))
            self.down = copy(src, near.at[1], 2, 3, jnp.maximum(z - 1, 0))
            self.out = [
                [copy(src.at[parts[h]], held.at[d], 4 + h, 6 + d, via[h]) for h in range(2)]
                for d in range(2)
            ]
            self.on = [
                [copy(held.at[d], near.at[d, parts[h]], 8 + d, 10 + h, middle - d) for h in range(2)]
                for d in range(2)
            ]

        def start(self):
            pl.when((z < owners - 1) & (z != middle - 1))(self.up.start)
            pl.when((z > 0) & (z != middle))(self.down.start)
            for d in range(2):
                for h in range(2):
                    pl.when(z == middle - 1 + d)(self.out[d][h].start)

        def forward(self):
            for h in range(2):
                @pl.when(z == via[h])
                def _():
                    for d in range(2):
                        self.out[d][h].wait_recv()
                        self.on[d][h].start()

        def wait(self):
            @pl.when((z < owners - 1) & (z != middle - 1))
            def _():
                self.up.wait_send()
                self.down.wait_recv()

            @pl.when((z > 0) & (z != middle))
            def _():
                self.down.wait_send()
                self.up.wait_recv()

            for d in range(2):
                @pl.when(z == middle - 1 + d)
                def _():
                    for h in range(2):
                        self.out[d][h].wait_send()
                        self.on[1 - d][h].wait_recv()

            for h in range(2):
                @pl.when(z == via[h])
                def _():
                    for d in range(2):
                        self.on[d][h].wait_send()

    def row_copies(buf, sems):
        after = remote(
            buf.at[pl.ds(rows, PAD)], buf.at[pl.ds(0, PAD)], sems.at[0],
            {"gx": jnp.minimum(g + 1, slabs - 1)},
        )
        before = remote(
            buf.at[pl.ds(PAD, PAD)], buf.at[pl.ds(PAD + rows, PAD)], sems.at[1],
            {"gx": jnp.maximum(g - 1, 0)},
        )
        return after, before

    def start_pair(pair, to_first, to_second):
        @pl.when(to_first)
        def _():
            pair[0].start()

        @pl.when(to_second)
        def _():
            pair[1].start()

    def wait_pair(pair, has_before, has_after):
        @pl.when(has_after)
        def _():
            pair[0].wait_send()
            pair[1].wait_recv()

        @pl.when(has_before)
        def _():
            pair[1].wait_send()
            pair[0].wait_recv()

    def clear_rows(buf):
        @pl.when(jnp.logical_not(has_prev))
        def _():
            buf[pl.ds(0, PAD)] = jnp.zeros((PAD, NY), jnp.float32)

        @pl.when(jnp.logical_not(has_next))
        def _():
            buf[pl.ds(PAD + rows, PAD)] = jnp.zeros((PAD, NY), jnp.float32)

    def clear_planes(near):
        @pl.when(jnp.logical_not(has_low))
        def _():
            near[0] = jnp.zeros((rows, NY), jnp.float32)

        @pl.when(jnp.logical_not(has_high))
        def _():
            near[1] = jnp.zeros((rows, NY), jnp.float32)

    held = side_rows(per_owner)
    per_tile = TILE // B
    brick_row = lax.broadcasted_iota(jnp.int32, (BR, B), 0)
    brick_lane = lax.broadcasted_iota(jnp.int32, (BR, B), 1)

    def place(first, n, carry):
        b = (n // per_tile) * y_bricks + first + n % per_tile
        owner = from_ref[b]
        p = place_ref[b]
        keep = fluid_ref[b]
        r0 = pl.multiple_of((b // y_bricks) * BR, BR)
        c0 = pl.multiple_of((b % y_bricks) * B, B)
        at = (pl.ds(r0, BR), pl.ds(c0, B))
        at_pad = (pl.ds(pl.multiple_of(r0 + PAD, PAD), BR), pl.ds(c0, B))
        root[at_pad] = main_ref[owner, p, 0] * keep
        accel_z[at] = main_ref[owner, p, 1] * keep
        source[at] = main_ref[owner, p, 2] * keep
        top = side_ref[owner, pl.ds(p, 1), :]
        bottom = side_ref[owner, pl.ds(held + p, 1), :]
        cols = side_ref[owner, 2 * held : 2 * held + BR, :]
        begin = jnp.sum(jnp.where(brick_lane == 2 * p, cols, 0.0), axis=1, keepdims=True)
        end = jnp.sum(jnp.where(brick_lane == 2 * p + 1, cols, 0.0), axis=1, keepdims=True)
        accel_x[at_pad] = keep * jnp.where(
            brick_row == 0, top, jnp.where(brick_row == BR - 1, bottom, 0.0)
        )
        accel_y[at] = keep * jnp.where(
            brick_lane == 0, begin, jnp.where(brick_lane == B - 1, end, 0.0)
        )
        fluid[at] = jnp.full((BR, B), keep, jnp.float32)
        return carry

    pieces = []
    for j in range(tiles):
        lax.fori_loop(
            0, rows // BR * per_tile, functools.partial(place, j * per_tile), 0, unroll=2
        )
        if j == 0:
            pl.semaphore_wait(barrier, owners + slabs - 2)
        at = pl.ds(j * TILE, TILE)
        pair = [
            Piece(root.at[pl.ds(PAD, rows), at], near_root.at[:, :, at], relay.at[j], near_sem.at[0, j]),
            Piece(accel_z.at[:, at], near_accel.at[:, :, at], relay.at[tiles + j], near_sem.at[1, j]),
        ]
        for piece in pair:
            piece.start()
        pieces.append(pair)
    row_pairs = [row_copies(root, row_sem.at[0]), row_copies(accel_x, row_sem.at[1])]
    for pair in row_pairs:
        start_pair(pair, has_next, has_prev)
    for buf in (root, accel_x, t_pad.at[0], t_pad.at[1]):
        clear_rows(buf)
    for piece in pieces[0]:
        piece.forward()
    for buf in (near_root, near_accel, near_t.at[0], near_t.at[1]):
        clear_planes(buf)
    for pair in row_pairs:
        wait_pair(pair, has_prev, has_next)

    row = lax.broadcasted_iota(jnp.int32, (CHUNK, NY), 0)
    lane = lax.broadcasted_iota(jnp.int32, (CHUNK, NY), 1)

    def left(value):
        return jnp.where(lane == 0, 0.0, pltpu.roll(value, 1, 1))

    def right(value):
        return jnp.where(lane == NY - 1, 0.0, pltpu.roll(value, NY - 1, 1))

    def at_chunk(i):
        r0 = pl.multiple_of(i * CHUNK, CHUNK)
        return pl.ds(r0, CHUNK), pl.ds(r0, CHUNK + 2 * PAD)

    def shifts(wide):
        return (
            wide[PAD - 1 : PAD - 1 + CHUNK],
            wide[PAD : PAD + CHUNK],
            wide[PAD + 1 : PAD + 1 + CHUNK],
        )

    def store_residual(at, cols, value):
        residual_ref[0, at, cols] = value
        high, low = split(value)
        res_hl[0, at, cols] = high
        res_hl[1, at, cols] = low

    def prepare(i, carry):
        at, wide_at = at_chunk(i)
        s_wide = root[wide_at, :]
        s_up, s, s_down = shifts(s_wide)
        ax_wide = accel_x[wide_at, :]
        ax = ax_wide[PAD : PAD + CHUNK]
        px_up, _, px_down = shifts(s_wide * ax_wide)
        ay = accel_y[at, :]
        py = s * ay
        s_left, s_right = left(s), right(s)
        total = jnp.where(row == 0, px_up + ax * s_up, 0.0)
        total = total - jnp.where(row == CHUNK - 1, px_down + ax * s_down, 0.0)
        total = total + jnp.where(lane % B == 0, left(py) + ay * s_left, 0.0)
        total = total - jnp.where(lane % B == B - 1, right(py) + ay * s_right, 0.0)
        source[at, :] = source[at, :] + 0.5 * s * total
        ring = s_up + s_down + s_left + s_right
        diagonal[at, :] = s * (shift_rate * s + ring) + (1.0 - fluid[at, :])
        return carry

    chunks = rows // CHUNK
    lax.fori_loop(0, chunks, prepare, 0)
    for pair in pieces[1:]:
        for piece in pair:
            piece.forward()
    for copy in table_copies:
        copy.wait()

    every = pl.ds(0, NY)

    def add_planes(cols, i, carry):
        at, _ = at_chunk(i)
        s = root[pl.ds(pl.multiple_of(i * CHUNK + PAD, PAD), CHUNK), cols]
        s_low, s_high = near_root[0, at, cols], near_root[1, at, cols]
        total = s_low * near_accel[0, at, cols] - s_high * near_accel[1, at, cols]
        total = total + accel_z[at, cols] * (s_low - s_high)
        store_residual(at, cols, source[at, cols] + 0.5 * s * total)
        diagonal[at, cols] = diagonal[at, cols] + s * (s_low + s_high)
        return carry

    def three(left_hl, right_hl):
        lh, ll = left_hl
        rh, rl = right_hl
        return dot32(lh, rh) + dot32(lh, rl) + dot32(ll, rh)

    def tile_at(j):
        return pl.ds(pl.multiple_of(j * TILE, TILE), TILE)

    def accumulate(j):
        cols = pl.ds(j * TILE, TILE)

        def one(k, carry):
            at = tile_at(k)
            lines = three((res_hl[0, :, cols], res_hl[1, :, cols]), (fwd[0, cols, at], fwd[1, cols, at]))
            if j:
                lines = spec[:, at] + lines
            spec[:, at] = lines
            return carry

        lax.fori_loop(0, tiles, one, 0)

    def precondition(it):
        def forward(j, carry):
            at = tile_at(j)
            modes = three((table_x[0], table_x[1]), split(spec[:, at])) * inverse_ref[:, at]
            spec[:, at] = modes
            edge[it, 0:1, at] = jnp.sum(modes * ends_ref[:, 0:1], axis=0, keepdims=True)
            edge[it, 1:2, at] = jnp.sum(modes * ends_ref[:, B : B + 1], axis=0, keepdims=True)
            return carry

        edge[it] = jnp.zeros((8, NY), jnp.float32)
        lax.fori_loop(0, tiles, forward, 0)
        copies = [
            remote(edge.at[it], gathered.at[it, g], edge_sem.at[it, k], {"gx": lax.rem(g + k, slabs)})
            for k in range(1, slabs)
        ]
        for copy in copies:
            copy.start()
        gathered[it, g] = edge[it]
        for copy in copies:
            copy.wait()
        sides = []
        for side in range(2):
            total = jnp.zeros((1, NY), jnp.float32)
            for j in range(slabs):
                for end in range(2):
                    n = 2 * j + end
                    total = total + couple_ref[g, side, n : n + 1, :] * gathered[it, j, end : end + 1, :]
            sides.append(total)
        edge_y = jnp.concatenate(sides, axis=0)
        part[0:2, :] = edge_y

        def back_x(j, carry):
            at = tile_at(j)
            fix = ends_ref[:, 0:1] * part[0:1, at] + ends_ref[:, B : B + 1] * part[1:2, at]
            modes = spec[:, at] + inverse_ref[:, at] * fix
            high, low = split(three((table_xt[0], table_xt[1]), split(modes)))
            x_hl[0, :, at] = high
            x_hl[1, :, at] = low
            return carry

        lax.fori_loop(0, tiles, back_x, 0)
        pairs = []
        for j in range(tiles):
            at = pl.ds(j * TILE, TILE)
            out = three((x_hl[0], x_hl[1]), (inv[0, :, at], inv[1, :, at])) * fluid[:, at]
            update[it, :, at] = out
            t_pad[it, pl.ds(PAD, rows), at] = out * root[pl.ds(PAD, rows), at]
            piece = Piece(
                t_pad.at[it, pl.ds(PAD, rows), at], near_t.at[it, :, :, at],
                relay.at[(2 + it) * tiles + j], t_sem.at[it, j],
            )
            piece.start()
            pairs.append(piece)
        rim = row_copies(t_pad.at[it], t_row_sem.at[it])
        start_pair(rim, has_next, has_prev)
        pairs[0].forward()
        wait_pair(rim, has_prev, has_next)
        return pairs

    def operate(it, pairs):
        def within(i, carry):
            at, wide_at = at_chunk(i)
            t_up, t, t_down = shifts(t_pad[it, wide_at, :])
            _, s, _ = shifts(root[wide_at, :])
            near = t_up + t_down + left(t) + right(t)
            image[it, at, :] = diagonal[at, :] * update[it, at, :] - s * near
            return carry

        lax.fori_loop(0, chunks, within, 0)
        for piece in pairs[1:]:
            piece.forward()

        def across(cols, i, carry):
            energy, curve = carry
            at, _ = at_chunk(i)
            s = root[pl.ds(pl.multiple_of(i * CHUNK + PAD, PAD), CHUNK), cols]
            u = update[it, at, cols]
            out = image[it, at, cols] - s * (near_t[it, 0, at, cols] + near_t[it, 1, at, cols])
            image[it, at, cols] = out
            return energy + u * residual_ref[0, at, cols], curve + u * out

        zero = jnp.zeros((CHUNK, TILE), jnp.float32)
        energy, curve = zero, zero
        for j in range(tiles):
            pairs[j].wait()
            energy, curve = lax.fori_loop(
                0, chunks, functools.partial(across, pl.ds(j * TILE, TILE)), (energy, curve)
            )
        part_row = lax.broadcasted_iota(jnp.int32, (8, B), 0)
        block = jnp.where(part_row < 4, jnp.sum(energy), jnp.sum(curve))
        for buf, sems, axis, count, index in (
            (total_yz, yz_sem, "yz", owners, z),
            (total_gx, gx_sem, "gx", slabs, g),
        ):
            buf[it, index] = block
            copies = [
                remote(buf.at[it, index], buf.at[it, index], sems.at[it, k], {axis: lax.rem(index + k, count)})
                for k in range(1, count)
            ]
            for copy in copies:
                copy.start()
            for copy in copies:
                copy.wait()
            block = buf[it, 0]
            for k in range(1, count):
                block = block + buf[it, k]
        return block[0:1, 0:1], block[4:5, 0:1]

    for j in range(tiles):
        for piece in pieces[j]:
            piece.wait()
        lax.fori_loop(0, chunks, functools.partial(add_planes, pl.ds(j * TILE, TILE)), 0)
        accumulate(j)
    energy_now, curvature = operate(0, precondition(0))
    step_now = energy_now / curvature

    def advance(i, carry):
        at, _ = at_chunk(i)
        store_residual(at, every, residual_ref[0, at, :] - step_now * image[0, at, :])
        return carry

    lax.fori_loop(0, chunks, advance, 0)
    for j in range(tiles):
        accumulate(j)
    energy_next, curvature = operate(1, precondition(1))
    beta = energy_next / energy_now
    step_next = energy_next / (curvature - beta * energy_next / step_now)

    def finish(i, carry):
        at, _ = at_chunk(i)
        first, second = update[0, at, :], update[1, at, :]
        solution_ref[0, at, :] = step_now * first + step_next * (second + beta * first)
        residual_ref[0, at, :] = residual_ref[0, at, :] - step_next * (
            image[1, at, :] + beta * image[0, at, :]
        )
        return carry

    lax.fori_loop(0, chunks, finish, 0)


def solve(owner_of, place_of, fluid, main, side, slabs, owners, rows, y_bricks):
    tables = [jnp.asarray(t) for t in solver_tables(slabs, rows)]
    plane = (rows, NY)
    padded = (rows + 2 * PAD, NY)
    f32, bf16 = jnp.float32, jnp.bfloat16
    vmem = pl.BlockSpec(memory_space=pltpu.VMEM)
    smem = pl.BlockSpec(memory_space=pltpu.SMEM)
    hbm = pl.BlockSpec(memory_space=pl.ANY)
    dma = pltpu.SemaphoreType.DMA
    out = jax.ShapeDtypeStruct((1,) + plane, f32)
    return pl.pallas_call(
        functools.partial(solver_kernel, slabs, owners, rows, y_bricks, main.shape[1]),
        out_shape=(out, out),
        in_specs=[smem] * 3 + [vmem, vmem, hbm, hbm] + [vmem] * 5,
        out_specs=(vmem, vmem),
        scratch_shapes=[
            pltpu.VMEM((2, NY, NY), bf16),
            pltpu.VMEM((2, NY, NY), bf16),
            pltpu.VMEM(padded, f32),
            pltpu.VMEM(padded, f32),
            pltpu.VMEM(plane, f32),
            pltpu.VMEM(plane, f32),
            pltpu.VMEM(plane, f32),
            pltpu.VMEM(plane, f32),
            pltpu.VMEM(plane, f32),
            pltpu.VMEM((2,) + plane, f32),
            pltpu.VMEM((2,) + plane, f32),
            pltpu.VMEM((ITERS, 2) + plane, f32),
            pltpu.VMEM((ITERS,) + padded, f32),
            pltpu.VMEM((2,) + plane, bf16),
            pltpu.VMEM(plane, f32),
            pltpu.VMEM((2,) + plane, bf16),
            pltpu.VMEM((ITERS,) + plane, f32),
            pltpu.VMEM((ITERS,) + plane, f32),
            pltpu.VMEM((ITERS, 8, NY), f32),
            pltpu.VMEM((ITERS, slabs, 8, NY), f32),
            pltpu.VMEM((8, NY), f32),
            pltpu.VMEM((ITERS, owners, 8, B), f32),
            pltpu.VMEM((ITERS, slabs, 8, B), f32),
            pltpu.VMEM(((2 + ITERS) * (NY // TILE), 2, rows // 2, TILE), f32),
            dma((2,)),
            dma((2, NY // TILE, 12)),
            dma((2, 2, 2)),
            dma((ITERS, NY // TILE, 12)),
            dma((ITERS, 2, 2)),
            dma((ITERS, slabs, 2)),
            dma((ITERS, owners, 2)),
            dma((ITERS, slabs, 2)),
        ],
        compiler_params=pltpu.CompilerParams(
            collective_id=1, has_side_effects=True, vmem_limit_bytes=60 * 2**20
        ),
        name="pressure_solver",
    )(owner_of, place_of, fluid, main, side, *tables)


def ranks_of(owners_of, owner_count):
    one_hot = (owners_of[..., None] == jnp.arange(owner_count, dtype=jnp.int32)).astype(jnp.int32)
    earlier = jnp.cumsum(one_hot, axis=-2) - one_hot
    return jnp.sum(earlier * one_hot, axis=-1)


def on_device(camera_accel, camera_weight, brick_slot, brick_solid):
    owner_count = lax.axis_size("yz")
    slabs = lax.axis_size("gx")
    slot_count = brick_slot.shape[1]
    per_owner = 3 * slot_count // (2 * owner_count)
    rows = NX // slabs
    y_bricks = NY // B
    slots = jnp.arange(slot_count, dtype=jnp.int32)

    brick_ids = brick_slot[0]
    owners_of = brick_ids // slot_count
    target = owners_of * per_owner + ranks_of(owners_of, owner_count)
    positions = jnp.arange(owner_count * per_owner, dtype=jnp.int32)
    matches = target[None, :] == positions[:, None]
    source = jnp.sum(jnp.where(matches, slots[None, :], 0), axis=1)

    found = jnp.sum(jnp.where(matches, 1 + brick_ids[None, :] % slot_count, 0), axis=1) - 1
    ids = jnp.pad(
        found.astype(jnp.float32).reshape(owner_count, 1, per_owner),
        ((0, 0), (0, 7), (0, B - per_owner)),
        constant_values=-1.0,
    )
    main, side = exchange(source, ids, camera_accel[0], camera_weight[0], owner_count, per_owner)
    held_ids = side[:, -8, :per_owner].reshape(-1)
    arrived = held_ids[None, :] == slots.astype(jnp.float32)[:, None]
    anchor = jnp.sum(jnp.where(arrived, positions[None, :], 0), axis=1)
    fluid = (1 - brick_solid[0]).astype(jnp.float32)
    return solve(
        anchor // per_owner, anchor % per_owner, fluid, main, side, slabs, owner_count, rows, y_bricks
    )


def solution(mesh):
    return jax.shard_map(
        on_device,
        mesh=mesh,
        in_specs=(
            P("gx", "yz", None, None, None),
            P("gx", "yz", None, None),
            P("gx", "yz"),
            P("gx", "yz"),
        ),
        out_specs=(P("yz", "gx", None), P("yz", "gx", None)),
        check_vma=False,
    )
```

```python
import functools

import jax
import jax.numpy as jnp
import ml_dtypes
import numpy as np
from jax import lax
from jax.experimental import pallas as pl
from jax.experimental.pallas import tpu as pltpu
from jax.sharding import PartitionSpec as P

NX = 1024
NY = 1024
BR = 16
B = 128
ITERS = 2

shift_rate = 0.05
spectral_gain = 1.0
spectral_floor = 2.0

MESH = pl.DeviceIdType.MESH
PAD = 8
CHUNK = BR
TILE = 256
WIDE = 512


def cosine_table(length):
    rows = np.arange(length, dtype=np.int64)[:, None]
    cols = np.arange(length, dtype=np.int64)[None, :]
    phases = (rows * (2 * cols + 1)) % (4 * length)
    scale = np.sqrt(np.where(rows == 0, 1.0, 2.0) / length)
    return scale * np.cos(phases * (np.pi / (2.0 * length)))


def eigen_values(length):
    return 2.0 - 2.0 * np.cos(np.arange(length) * (np.pi / length))


def high_low(table):
    high = table.astype(np.float32).astype(ml_dtypes.bfloat16)
    low = (table - high.astype(np.float64)).astype(np.float32).astype(ml_dtypes.bfloat16)
    return np.stack([high, low])


def solver_tables(slabs, rows):
    table_y = cosine_table(NY)
    table_x = cosine_table(rows)
    inverse = 1.0 / (
        spectral_gain * (eigen_values(rows)[:, None] + eigen_values(NY)[None, :]) + spectral_floor
    )
    first, last = table_x[:, :1], table_x[:, -1:]
    same = np.sum(first * first * inverse, axis=0)
    cross = np.sum(first * last * inverse, axis=0)
    faces = slabs - 1
    couple = np.zeros((slabs, 2, 2 * slabs, NY))
    if faces:
        matrix = np.zeros((NY, faces, faces))
        for i in range(faces):
            matrix[:, i, i] = 1.0 / spectral_gain + 2.0 * same
            if i:
                matrix[:, i, i - 1] = matrix[:, i - 1, i] = -cross
        solved = np.linalg.inv(matrix)
        for slab in range(slabs):
            for side, face, sign in ((0, slab - 1, 1.0), (1, slab, -1.0)):
                if 0 <= face < faces:
                    for other in range(faces):
                        couple[slab, side, 2 * other + 1] += sign * solved[:, face, other]
                        couple[slab, side, 2 * other + 2] -= sign * solved[:, face, other]
    ends = np.concatenate([np.repeat(first, B, 1), np.repeat(last, B, 1)], axis=1)
    return (
        high_low(table_y.T),
        high_low(table_y),
        high_low(table_x),
        high_low(table_x.T),
        inverse.astype(np.float32),
        ends.astype(np.float32),
        couple.astype(np.float32),
    )


def partner(me, k, owners):
    total, bit = 0, 1
    while bit < owners:
        digit = (me // bit) % 2
        total = total + bit * (1 - digit if k & bit else digit)
        bit *= 2
    return total


def partner_order(owners):
    far = [k for k in range(owners - 1, 1, -1) if k % 2 == 0]
    return far + [k + 1 for k in far] + [1]


def exchange_kernel(
    owners, per_owner, src_ref, ids_ref, accel_ref, weight_ref, main_out, side_out,
    main, side, main_send, main_recv, side_send, side_recv,
):
    me = lax.axis_index("yz")
    barrier = pltpu.get_barrier_semaphore()
    for k in range(1, owners):
        pl.semaphore_signal(
            barrier, inc=1, device_id={"yz": lax.rem(me + k, owners)}, device_id_type=MESH
        )
    row_cells, col_cells = weight_ref.shape[1:]
    row = lax.broadcasted_iota(jnp.int32, (row_cells, col_cells), 0)
    lane = lax.broadcasted_iota(jnp.int32, (row_cells, col_cells), 1)
    held = side_rows(per_owner)

    def pack(k, owner):
        def one(p, cols):
            slot = src_ref[owner * per_owner + p]
            root = jnp.sqrt(weight_ref[slot])
            ax, ay = accel_ref[slot, 1], accel_ref[slot, 2]
            px, py = root * ax, root * ay
            s_up = jnp.where(row == 0, 0.0, pltpu.roll(root, 1, 0))
            s_down = jnp.where(row == row_cells - 1, 0.0, pltpu.roll(root, row_cells - 1, 0))
            s_left = jnp.where(lane == 0, 0.0, pltpu.roll(root, 1, 1))
            s_right = jnp.where(lane == col_cells - 1, 0.0, pltpu.roll(root, col_cells - 1, 1))
            p_up = jnp.where(row == 0, 0.0, pltpu.roll(px, 1, 0))
            p_down = jnp.where(row == row_cells - 1, 0.0, pltpu.roll(px, row_cells - 1, 0))
            p_left = jnp.where(lane == 0, 0.0, pltpu.roll(py, 1, 1))
            p_right = jnp.where(lane == col_cells - 1, 0.0, pltpu.roll(py, col_cells - 1, 1))
            total = p_up - p_down + p_left - p_right + ax * (s_up - s_down) + ay * (s_left - s_right)
            main[k, p, 0] = root
            main[k, p, 1] = accel_ref[slot, 0]
            main[k, p, 2] = 0.5 * root * total
            side[k, pl.ds(p, 1), :] = ax[0:1]
            side[k, pl.ds(held + p, 1), :] = ax[row_cells - 1 : row_cells]
            cols = jnp.where(lane == 2 * p, ay[:, 0:1], cols)
            return jnp.where(lane == 2 * p + 1, ay[:, col_cells - 1 : col_cells], cols)

        cols = lax.fori_loop(0, per_owner, one, jnp.zeros((row_cells, col_cells), jnp.float32))
        side[k, 2 * held : 2 * held + row_cells, :] = cols
        side[k, 2 * held + row_cells :, :] = ids_ref[owner]

    side[...] = jnp.zeros_like(side)
    copies = []
    for count, k in enumerate(partner_order(owners)):
        owner = partner(me, k, owners)
        pack(k, owner)
        if count == 0:
            pl.semaphore_wait(barrier, owners - 1)
        for src, dst, send, recv in (
            (main, main_out, main_send, main_recv),
            (side, side_out, side_send, side_recv),
        ):
            copy = pltpu.make_async_remote_copy(
                src_ref=src.at[k],
                dst_ref=dst.at[me],
                send_sem=send.at[k],
                recv_sem=recv.at[k],
                device_id={"yz": owner},
                device_id_type=MESH,
            )
            copy.start()
            copies.append(copy)
    pack(0, me)
    own = [
        pltpu.make_async_copy(main.at[0], main_out.at[me], main_send.at[0]),
        pltpu.make_async_copy(side.at[0], side_out.at[me], side_send.at[0]),
    ]
    for copy in own:
        copy.start()
    for copy in own:
        copy.wait()
    for copy in copies:
        copy.wait()


def side_rows(per_owner):
    return -(-per_owner // 8) * 8


def exchange(source, ids, accel, weight, owners, per_owner):
    slots, _, row_cells, col_cells = accel.shape
    main_shape = (owners, per_owner, 3, row_cells, col_cells)
    side_shape = (owners, 2 * side_rows(per_owner) + row_cells + 8, col_cells)
    return pl.pallas_call(
        functools.partial(exchange_kernel, owners, per_owner),
        out_shape=(
            jax.ShapeDtypeStruct(main_shape, jnp.float32),
            jax.ShapeDtypeStruct(side_shape, jnp.float32),
        ),
        in_specs=[pl.BlockSpec(memory_space=pltpu.SMEM)] + [pl.BlockSpec(memory_space=pltpu.VMEM)] * 3,
        out_specs=(pl.BlockSpec(memory_space=pl.ANY), pl.BlockSpec(memory_space=pl.ANY)),
        scratch_shapes=[
            pltpu.VMEM(main_shape, jnp.float32),
            pltpu.VMEM(side_shape, jnp.float32),
        ]
        + [pltpu.SemaphoreType.DMA((owners,))] * 4,
        compiler_params=pltpu.CompilerParams(
            collective_id=0, has_side_effects=True, vmem_limit_bytes=40 * 2**20
        ),
        name="brick_exchange",
    )(source, ids, accel, weight)


def split(value):
    high = value.astype(jnp.bfloat16)
    return high, (value - high.astype(jnp.float32)).astype(jnp.bfloat16)


def dot32(left, right):
    return jnp.dot(left, right, preferred_element_type=jnp.float32)


def solver_kernel(
    slabs, owners, rows, y_bricks, per_owner,
    from_ref, place_ref, fluid_ref, main_ref, side_ref, fwd_hbm, inv_hbm, table_x, table_xt, inverse_ref, ends_ref, couple_ref,
    solution_ref, residual_ref,
    fwd, inv, root, accel_x, accel_y, accel_z, source, fluid, diagonal, near_root, near_accel, near_t, t_pad,
    res_hl, spec, x_hl, update, image, edge, gathered, part, total_yz, total_gx, relay,
    table_sem, near_sem, row_sem, t_sem, t_row_sem, edge_sem, yz_sem, gx_sem,
):
    g = lax.axis_index("gx")
    z = lax.axis_index("yz")
    barrier = pltpu.get_barrier_semaphore()
    for k in range(1, owners):
        pl.semaphore_signal(barrier, inc=1, device_id={"yz": lax.rem(z + k, owners)}, device_id_type=MESH)
    for k in range(1, slabs):
        pl.semaphore_signal(barrier, inc=1, device_id={"gx": lax.rem(g + k, slabs)}, device_id_type=MESH)

    table_copies = [
        pltpu.make_async_copy(fwd_hbm, fwd, table_sem.at[0]),
        pltpu.make_async_copy(inv_hbm, inv, table_sem.at[1]),
    ]
    for copy in table_copies:
        copy.start()

    has_low, has_high = z > 0, z < owners - 1
    has_prev, has_next = g > 0, g < slabs - 1

    def remote(src, dst, sems, device):
        return pltpu.make_async_remote_copy(
            src_ref=src, dst_ref=dst, send_sem=sems.at[0], recv_sem=sems.at[1],
            device_id=device, device_id_type=MESH,
        )

    half = rows // 2
    middle = owners // 2
    via = (0, owners - 1)
    tiles = NY // TILE

    class Piece:
        def __init__(self, src, near, held, sems):
            parts = [pl.ds(0, half), pl.ds(half, half)]

            def copy(src, dst, send, recv, device):
                return pltpu.make_async_remote_copy(
                    src_ref=src, dst_ref=dst, send_sem=sems.at[send], recv_sem=sems.at[recv],
                    device_id={"yz": device}, device_id_type=MESH,
                )

            self.up = copy(src, near.at[0], 0, 1, jnp.minimum(z + 1, owners - 1))
            self.down = copy(src, near.at[1], 2, 3, jnp.maximum(z - 1, 0))
            self.out = [
                [copy(src.at[parts[h]], held.at[d], 4 + h, 6 + d, via[h]) for h in range(2)]
                for d in range(2)
            ]
            self.on = [
                [copy(held.at[d], near.at[d, parts[h]], 8 + d, 10 + h, middle - d) for h in range(2)]
                for d in range(2)
            ]

        def start(self):
            pl.when((z < owners - 1) & (z != middle - 1))(self.up.start)
            pl.when((z > 0) & (z != middle))(self.down.start)
            for d in range(2):
                for h in range(2):
                    pl.when(z == middle - 1 + d)(self.out[d][h].start)

        def forward(self):
            for h in range(2):
                @pl.when(z == via[h])
                def _():
                    for d in range(2):
                        self.out[d][h].wait_recv()
                        self.on[d][h].start()

        def wait(self):
            @pl.when((z < owners - 1) & (z != middle - 1))
            def _():
                self.up.wait_send()
                self.down.wait_recv()

            @pl.when((z > 0) & (z != middle))
            def _():
                self.down.wait_send()
                self.up.wait_recv()

            for d in range(2):
                @pl.when(z == middle - 1 + d)
                def _():
                    for h in range(2):
                        self.out[d][h].wait_send()
                        self.on[1 - d][h].wait_recv()

            for h in range(2):
                @pl.when(z == via[h])
                def _():
                    for d in range(2):
                        self.on[d][h].wait_send()

    def row_copies(buf, sems):
        after = remote(
            buf.at[pl.ds(rows, PAD)], buf.at[pl.ds(0, PAD)], sems.at[0],
            {"gx": jnp.minimum(g + 1, slabs - 1)},
        )
        before = remote(
            buf.at[pl.ds(PAD, PAD)], buf.at[pl.ds(PAD + rows, PAD)], sems.at[1],
            {"gx": jnp.maximum(g - 1, 0)},
        )
        return after, before

    def start_pair(pair, to_first, to_second):
        @pl.when(to_first)
        def _():
            pair[0].start()

        @pl.when(to_second)
        def _():
            pair[1].start()

    def wait_pair(pair, has_before, has_after):
        @pl.when(has_after)
        def _():
            pair[0].wait_send()
            pair[1].wait_recv()

        @pl.when(has_before)
        def _():
            pair[1].wait_send()
            pair[0].wait_recv()

    def clear_rows(buf):
        @pl.when(jnp.logical_not(has_prev))
        def _():
            buf[pl.ds(0, PAD)] = jnp.zeros((PAD, NY), jnp.float32)

        @pl.when(jnp.logical_not(has_next))
        def _():
            buf[pl.ds(PAD + rows, PAD)] = jnp.zeros((PAD, NY), jnp.float32)

    def clear_planes(near):
        @pl.when(jnp.logical_not(has_low))
        def _():
            near[0] = jnp.zeros((rows, NY), jnp.float32)

        @pl.when(jnp.logical_not(has_high))
        def _():
            near[1] = jnp.zeros((rows, NY), jnp.float32)

    held = side_rows(per_owner)
    per_tile = TILE // B
    brick_row = lax.broadcasted_iota(jnp.int32, (BR, B), 0)
    brick_lane = lax.broadcasted_iota(jnp.int32, (BR, B), 1)

    def place(first, n, carry):
        b = (n // per_tile) * y_bricks + first + n % per_tile
        owner = from_ref[b]
        p = place_ref[b]
        keep = fluid_ref[b]
        r0 = pl.multiple_of((b // y_bricks) * BR, BR)
        c0 = pl.multiple_of((b % y_bricks) * B, B)
        at = (pl.ds(r0, BR), pl.ds(c0, B))
        at_pad = (pl.ds(pl.multiple_of(r0 + PAD, PAD), BR), pl.ds(c0, B))
        root[at_pad] = main_ref[owner, p, 0] * keep
        accel_z[at] = main_ref[owner, p, 1] * keep
        source[at] = main_ref[owner, p, 2] * keep
        top = side_ref[owner, pl.ds(p, 1), :]
        bottom = side_ref[owner, pl.ds(held + p, 1), :]
        cols = side_ref[owner, 2 * held : 2 * held + BR, :]
        begin = jnp.sum(jnp.where(brick_lane == 2 * p, cols, 0.0), axis=1, keepdims=True)
        end = jnp.sum(jnp.where(brick_lane == 2 * p + 1, cols, 0.0), axis=1, keepdims=True)
        accel_x[at_pad] = keep * jnp.where(
            brick_row == 0, top, jnp.where(brick_row == BR - 1, bottom, 0.0)
        )
        accel_y[at] = keep * jnp.where(
            brick_lane == 0, begin, jnp.where(brick_lane == B - 1, end, 0.0)
        )
        fluid[at] = jnp.full((BR, B), keep, jnp.float32)
        return carry

    pieces = []
    for j in range(tiles):
        lax.fori_loop(
            0, rows // BR * per_tile, functools.partial(place, j * per_tile), 0, unroll=2
        )
        if j == 0:
            pl.semaphore_wait(barrier, owners + slabs - 2)
        at = pl.ds(j * TILE, TILE)
        pair = [
            Piece(root.at[pl.ds(PAD, rows), at], near_root.at[:, :, at], relay.at[j], near_sem.at[0, j]),
            Piece(accel_z.at[:, at], near_accel.at[:, :, at], relay.at[tiles + j], near_sem.at[1, j]),
        ]
        for piece in pair:
            piece.start()
        pieces.append(pair)
    row_pairs = [row_copies(root, row_sem.at[0]), row_copies(accel_x, row_sem.at[1])]
    for pair in row_pairs:
        start_pair(pair, has_next, has_prev)
    for buf in (root, accel_x, t_pad.at[0], t_pad.at[1]):
        clear_rows(buf)
    for piece in pieces[0]:
        piece.forward()
    for buf in (near_root, near_accel, near_t.at[0], near_t.at[1]):
        clear_planes(buf)
    for pair in row_pairs:
        wait_pair(pair, has_prev, has_next)

    row = lax.broadcasted_iota(jnp.int32, (CHUNK, NY), 0)
    lane = lax.broadcasted_iota(jnp.int32, (CHUNK, NY), 1)

    def left(value):
        return jnp.where(lane == 0, 0.0, pltpu.roll(value, 1, 1))

    def right(value):
        return jnp.where(lane == NY - 1, 0.0, pltpu.roll(value, NY - 1, 1))

    def at_chunk(i):
        r0 = pl.multiple_of(i * CHUNK, CHUNK)
        return pl.ds(r0, CHUNK), pl.ds(r0, CHUNK + 2 * PAD)

    def shifts(wide):
        return (
            wide[PAD - 1 : PAD - 1 + CHUNK],
            wide[PAD : PAD + CHUNK],
            wide[PAD + 1 : PAD + 1 + CHUNK],
        )

    def store_residual(at, cols, value):
        residual_ref[0, at, cols] = value
        high, low = split(value)
        res_hl[0, at, cols] = high
        res_hl[1, at, cols] = low

    def prepare(i, carry):
        at, wide_at = at_chunk(i)
        s_wide = root[wide_at, :]
        s_up, s, s_down = shifts(s_wide)
        ax_wide = accel_x[wide_at, :]
        ax = ax_wide[PAD : PAD + CHUNK]
        px_up, _, px_down = shifts(s_wide * ax_wide)
        ay = accel_y[at, :]
        py = s * ay
        s_left, s_right = left(s), right(s)
        total = jnp.where(row == 0, px_up + ax * s_up, 0.0)
        total = total - jnp.where(row == CHUNK - 1, px_down + ax * s_down, 0.0)
        total = total + jnp.where(lane % B == 0, left(py) + ay * s_left, 0.0)
        total = total - jnp.where(lane % B == B - 1, right(py) + ay * s_right, 0.0)
        source[at, :] = source[at, :] + 0.5 * s * total
        ring = s_up + s_down + s_left + s_right
        diagonal[at, :] = s * (shift_rate * s + ring) + (1.0 - fluid[at, :])
        return carry

    chunks = rows // CHUNK
    lax.fori_loop(0, chunks, prepare, 0)
    for pair in pieces[1:]:
        for piece in pair:
            piece.forward()
    for copy in table_copies:
        copy.wait()

    every = pl.ds(0, NY)

    def add_planes(cols, i, carry):
        at, _ = at_chunk(i)
        s = root[pl.ds(pl.multiple_of(i * CHUNK + PAD, PAD), CHUNK), cols]
        s_low, s_high = near_root[0, at, cols], near_root[1, at, cols]
        total = s_low * near_accel[0, at, cols] - s_high * near_accel[1, at, cols]
        total = total + accel_z[at, cols] * (s_low - s_high)
        store_residual(at, cols, source[at, cols] + 0.5 * s * total)
        diagonal[at, cols] = diagonal[at, cols] + s * (s_low + s_high)
        return carry

    def three(left_hl, right_hl):
        lh, ll = left_hl
        rh, rl = right_hl
        return dot32(lh, rh) + dot32(lh, rl) + dot32(ll, rh)

    def tile_at(j):
        return pl.ds(pl.multiple_of(j * WIDE, WIDE), WIDE)

    def accumulate(j):
        cols = pl.ds(j * TILE, TILE)

        def one(k, carry):
            at = tile_at(k)
            lines = three((res_hl[0, :, cols], res_hl[1, :, cols]), (fwd[0, cols, at], fwd[1, cols, at]))
            if j:
                lines = spec[:, at] + lines
            spec[:, at] = lines
            return carry

        lax.fori_loop(0, NY // WIDE, one, 0)

    def precondition(it):
        def forward(j, carry):
            at = tile_at(j)
            if it:
                lines = three((res_hl[0], res_hl[1]), (fwd[0, :, at], fwd[1, :, at]))
            else:
                lines = spec[:, at]
            modes = three((table_x[0], table_x[1]), split(lines)) * inverse_ref[:, at]
            spec[:, at] = modes
            edge[it, 0:1, at] = jnp.sum(modes * ends_ref[:, 0:1], axis=0, keepdims=True)
            edge[it, 1:2, at] = jnp.sum(modes * ends_ref[:, B : B + 1], axis=0, keepdims=True)
            return carry

        edge[it] = jnp.zeros((8, NY), jnp.float32)
        lax.fori_loop(0, NY // WIDE, forward, 0)
        copies = [
            remote(edge.at[it], gathered.at[it, g], edge_sem.at[it, k], {"gx": lax.rem(g + k, slabs)})
            for k in range(1, slabs)
        ]
        for copy in copies:
            copy.start()
        gathered[it, g] = edge[it]
        for copy in copies:
            copy.wait()
        sides = []
        for side in range(2):
            total = jnp.zeros((1, NY), jnp.float32)
            for j in range(slabs):
                for end in range(2):
                    n = 2 * j + end
                    total = total + couple_ref[g, side, n : n + 1, :] * gathered[it, j, end : end + 1, :]
            sides.append(total)
        edge_y = jnp.concatenate(sides, axis=0)
        part[0:2, :] = edge_y

        def back_x(j, carry):
            at = tile_at(j)
            fix = ends_ref[:, 0:1] * part[0:1, at] + ends_ref[:, B : B + 1] * part[1:2, at]
            modes = spec[:, at] + inverse_ref[:, at] * fix
            high, low = split(three((table_xt[0], table_xt[1]), split(modes)))
            x_hl[0, :, at] = high
            x_hl[1, :, at] = low
            return carry

        lax.fori_loop(0, NY // WIDE, back_x, 0)
        pairs = []
        for j in range(tiles):
            at = pl.ds(j * TILE, TILE)
            out = three((x_hl[0], x_hl[1]), (inv[0, :, at], inv[1, :, at])) * fluid[:, at]
            update[it, :, at] = out
            t_pad[it, pl.ds(PAD, rows), at] = out * root[pl.ds(PAD, rows), at]
            piece = Piece(
                t_pad.at[it, pl.ds(PAD, rows), at], near_t.at[it, :, :, at],
                relay.at[(2 + it) * tiles + j], t_sem.at[it, j],
            )
            piece.start()
            pairs.append(piece)
        rim = row_copies(t_pad.at[it], t_row_sem.at[it])
        start_pair(rim, has_next, has_prev)
        pairs[0].forward()
        wait_pair(rim, has_prev, has_next)
        return pairs

    def operate(it, pairs):
        def within(i, carry):
            at, wide_at = at_chunk(i)
            t_up, t, t_down = shifts(t_pad[it, wide_at, :])
            _, s, _ = shifts(root[wide_at, :])
            near = t_up + t_down + left(t) + right(t)
            image[it, at, :] = diagonal[at, :] * update[it, at, :] - s * near
            return carry

        lax.fori_loop(0, chunks, within, 0)
        for piece in pairs[1:]:
            piece.forward()

        def across(cols, i, carry):
            energy, curve = carry
            at, _ = at_chunk(i)
            s = root[pl.ds(pl.multiple_of(i * CHUNK + PAD, PAD), CHUNK), cols]
            u = update[it, at, cols]
            out = image[it, at, cols] - s * (near_t[it, 0, at, cols] + near_t[it, 1, at, cols])
            image[it, at, cols] = out
            return energy + u * residual_ref[0, at, cols], curve + u * out

        zero = jnp.zeros((CHUNK, TILE), jnp.float32)
        energy, curve = zero, zero
        for j in range(tiles):
            pairs[j].wait()
            energy, curve = lax.fori_loop(
                0, chunks, functools.partial(across, pl.ds(j * TILE, TILE)), (energy, curve)
            )
        part_row = lax.broadcasted_iota(jnp.int32, (8, B), 0)
        block = jnp.where(part_row < 4, jnp.sum(energy), jnp.sum(curve))
        for buf, sems, axis, count, index in (
            (total_yz, yz_sem, "yz", owners, z),
            (total_gx, gx_sem, "gx", slabs, g),
        ):
            buf[it, index] = block
            copies = [
                remote(buf.at[it, index], buf.at[it, index], sems.at[it, k], {axis: lax.rem(index + k, count)})
                for k in range(1, count)
            ]
            for copy in copies:
                copy.start()
            for copy in copies:
                copy.wait()
            block = buf[it, 0]
            for k in range(1, count):
                block = block + buf[it, k]
        return block[0:1, 0:1], block[4:5, 0:1]

    for j in range(tiles):
        for piece in pieces[j]:
            piece.wait()
        lax.fori_loop(0, chunks, functools.partial(add_planes, pl.ds(j * TILE, TILE)), 0)
        accumulate(j)
    energy_now, curvature = operate(0, precondition(0))
    step_now = energy_now / curvature

    def advance(i, carry):
        at, _ = at_chunk(i)
        store_residual(at, every, residual_ref[0, at, :] - step_now * image[0, at, :])
        return carry

    lax.fori_loop(0, chunks, advance, 0)
    energy_next, curvature = operate(1, precondition(1))
    beta = energy_next / energy_now
    step_next = energy_next / (curvature - beta * energy_next / step_now)

    def finish(i, carry):
        at, _ = at_chunk(i)
        first, second = update[0, at, :], update[1, at, :]
        solution_ref[0, at, :] = step_now * first + step_next * (second + beta * first)
        residual_ref[0, at, :] = residual_ref[0, at, :] - step_next * (
            image[1, at, :] + beta * image[0, at, :]
        )
        return carry

    lax.fori_loop(0, chunks, finish, 0)


def solve(owner_of, place_of, fluid, main, side, slabs, owners, rows, y_bricks):
    tables = [jnp.asarray(t) for t in solver_tables(slabs, rows)]
    plane = (rows, NY)
    padded = (rows + 2 * PAD, NY)
    f32, bf16 = jnp.float32, jnp.bfloat16
    vmem = pl.BlockSpec(memory_space=pltpu.VMEM)
    smem = pl.BlockSpec(memory_space=pltpu.SMEM)
    hbm = pl.BlockSpec(memory_space=pl.ANY)
    dma = pltpu.SemaphoreType.DMA
    out = jax.ShapeDtypeStruct((1,) + plane, f32)
    return pl.pallas_call(
        functools.partial(solver_kernel, slabs, owners, rows, y_bricks, main.shape[1]),
        out_shape=(out, out),
        in_specs=[smem] * 3 + [vmem, vmem, hbm, hbm] + [vmem] * 5,
        out_specs=(vmem, vmem),
        scratch_shapes=[
            pltpu.VMEM((2, NY, NY), bf16),
            pltpu.VMEM((2, NY, NY), bf16),
            pltpu.VMEM(padded, f32),
            pltpu.VMEM(padded, f32),
            pltpu.VMEM(plane, f32),
            pltpu.VMEM(plane, f32),
            pltpu.VMEM(plane, f32),
            pltpu.VMEM(plane, f32),
            pltpu.VMEM(plane, f32),
            pltpu.VMEM((2,) + plane, f32),
            pltpu.VMEM((2,) + plane, f32),
            pltpu.VMEM((ITERS, 2) + plane, f32),
            pltpu.VMEM((ITERS,) + padded, f32),
            pltpu.VMEM((2,) + plane, bf16),
            pltpu.VMEM(plane, f32),
            pltpu.VMEM((2,) + plane, bf16),
            pltpu.VMEM((ITERS,) + plane, f32),
            pltpu.VMEM((ITERS,) + plane, f32),
            pltpu.VMEM((ITERS, 8, NY), f32),
            pltpu.VMEM((ITERS, slabs, 8, NY), f32),
            pltpu.VMEM((8, NY), f32),
            pltpu.VMEM((ITERS, owners, 8, B), f32),
            pltpu.VMEM((ITERS, slabs, 8, B), f32),
            pltpu.VMEM(((2 + ITERS) * (NY // TILE), 2, rows // 2, TILE), f32),
            dma((2,)),
            dma((2, NY // TILE, 12)),
            dma((2, 2, 2)),
            dma((ITERS, NY // TILE, 12)),
            dma((ITERS, 2, 2)),
            dma((ITERS, slabs, 2)),
            dma((ITERS, owners, 2)),
            dma((ITERS, slabs, 2)),
        ],
        compiler_params=pltpu.CompilerParams(
            collective_id=1, has_side_effects=True, vmem_limit_bytes=60 * 2**20
        ),
        name="pressure_solver",
    )(owner_of, place_of, fluid, main, side, *tables)


def ranks_of(owners_of, owner_count):
    one_hot = (owners_of[..., None] == jnp.arange(owner_count, dtype=jnp.int32)).astype(jnp.int32)
    earlier = jnp.cumsum(one_hot, axis=-2) - one_hot
    return jnp.sum(earlier * one_hot, axis=-1)


def on_device(camera_accel, camera_weight, brick_slot, brick_solid):
    owner_count = lax.axis_size("yz")
    slabs = lax.axis_size("gx")
    slot_count = brick_slot.shape[1]
    per_owner = 3 * slot_count // (2 * owner_count)
    rows = NX // slabs
    y_bricks = NY // B
    slots = jnp.arange(slot_count, dtype=jnp.int32)

    brick_ids = brick_slot[0]
    owners_of = brick_ids // slot_count
    target = owners_of * per_owner + ranks_of(owners_of, owner_count)
    positions = jnp.arange(owner_count * per_owner, dtype=jnp.int32)
    matches = target[None, :] == positions[:, None]
    source = jnp.sum(jnp.where(matches, slots[None, :], 0), axis=1)

    found = jnp.sum(jnp.where(matches, 1 + brick_ids[None, :] % slot_count, 0), axis=1) - 1
    ids = jnp.pad(
        found.astype(jnp.float32).reshape(owner_count, 1, per_owner),
        ((0, 0), (0, 7), (0, B - per_owner)),
        constant_values=-1.0,
    )
    main, side = exchange(source, ids, camera_accel[0], camera_weight[0], owner_count, per_owner)
    held_ids = side[:, -8, :per_owner].reshape(-1)
    arrived = held_ids[None, :] == slots.astype(jnp.float32)[:, None]
    anchor = jnp.sum(jnp.where(arrived, positions[None, :], 0), axis=1)
    fluid = (1 - brick_solid[0]).astype(jnp.float32)
    return solve(
        anchor // per_owner, anchor % per_owner, fluid, main, side, slabs, owner_count, rows, y_bricks
    )


def solution(mesh):
    return jax.shard_map(
        on_device,
        mesh=mesh,
        in_specs=(
            P("gx", "yz", None, None, None),
            P("gx", "yz", None, None),
            P("gx", "yz"),
            P("gx", "yz"),
        ),
        out_specs=(P("yz", "gx", None), P("yz", "gx", None)),
        check_vma=False,
    )
```

```python
import functools

import jax
import jax.numpy as jnp
import ml_dtypes
import numpy as np
from jax import lax
from jax.experimental import pallas as pl
from jax.experimental.pallas import tpu as pltpu
from jax.sharding import PartitionSpec as P

NX = 1024
NY = 1024
BR = 16
B = 128
ITERS = 2

shift_rate = 0.05
spectral_gain = 1.0
spectral_floor = 2.0

MESH = pl.DeviceIdType.MESH
PAD = 8
CHUNK = BR
TILE = 256
WIDE = 1024


def cosine_table(length):
    rows = np.arange(length, dtype=np.int64)[:, None]
    cols = np.arange(length, dtype=np.int64)[None, :]
    phases = (rows * (2 * cols + 1)) % (4 * length)
    scale = np.sqrt(np.where(rows == 0, 1.0, 2.0) / length)
    return scale * np.cos(phases * (np.pi / (2.0 * length)))


def eigen_values(length):
    return 2.0 - 2.0 * np.cos(np.arange(length) * (np.pi / length))


def high_low(table):
    high = table.astype(np.float32).astype(ml_dtypes.bfloat16)
    low = (table - high.astype(np.float64)).astype(np.float32).astype(ml_dtypes.bfloat16)
    return np.stack([high, low])


def solver_tables(slabs, rows):
    table_y = cosine_table(NY)
    table_x = cosine_table(rows)
    inverse = 1.0 / (
        spectral_gain * (eigen_values(rows)[:, None] + eigen_values(NY)[None, :]) + spectral_floor
    )
    first, last = table_x[:, :1], table_x[:, -1:]
    same = np.sum(first * first * inverse, axis=0)
    cross = np.sum(first * last * inverse, axis=0)
    faces = slabs - 1
    couple = np.zeros((slabs, 2, 2 * slabs, NY))
    if faces:
        matrix = np.zeros((NY, faces, faces))
        for i in range(faces):
            matrix[:, i, i] = 1.0 / spectral_gain + 2.0 * same
            if i:
                matrix[:, i, i - 1] = matrix[:, i - 1, i] = -cross
        solved = np.linalg.inv(matrix)
        for slab in range(slabs):
            for side, face, sign in ((0, slab - 1, 1.0), (1, slab, -1.0)):
                if 0 <= face < faces:
                    for other in range(faces):
                        couple[slab, side, 2 * other + 1] += sign * solved[:, face, other]
                        couple[slab, side, 2 * other + 2] -= sign * solved[:, face, other]
    ends = np.concatenate([np.repeat(first, B, 1), np.repeat(last, B, 1)], axis=1)
    return (
        high_low(table_y.T),
        high_low(table_y),
        high_low(table_x),
        high_low(table_x.T),
        inverse.astype(np.float32),
        ends.astype(np.float32),
        couple.astype(np.float32),
    )


def partner(me, k, owners):
    total, bit = 0, 1
    while bit < owners:
        digit = (me // bit) % 2
        total = total + bit * (1 - digit if k & bit else digit)
        bit *= 2
    return total


def partner_order(owners):
    far = [k for k in range(owners - 1, 1, -1) if k % 2 == 0]
    return far + [k + 1 for k in far] + [1]


def exchange_kernel(
    owners, per_owner, src_ref, ids_ref, accel_ref, weight_ref, main_out, side_out,
    main, side, main_send, main_recv, side_send, side_recv,
):
    me = lax.axis_index("yz")
    barrier = pltpu.get_barrier_semaphore()
    for k in range(1, owners):
        pl.semaphore_signal(
            barrier, inc=1, device_id={"yz": lax.rem(me + k, owners)}, device_id_type=MESH
        )
    row_cells, col_cells = weight_ref.shape[1:]
    row = lax.broadcasted_iota(jnp.int32, (row_cells, col_cells), 0)
    lane = lax.broadcasted_iota(jnp.int32, (row_cells, col_cells), 1)
    held = side_rows(per_owner)

    def pack(k, owner):
        def one(p, cols):
            slot = src_ref[owner * per_owner + p]
            root = jnp.sqrt(weight_ref[slot])
            ax, ay = accel_ref[slot, 1], accel_ref[slot, 2]
            px, py = root * ax, root * ay
            s_up = jnp.where(row == 0, 0.0, pltpu.roll(root, 1, 0))
            s_down = jnp.where(row == row_cells - 1, 0.0, pltpu.roll(root, row_cells - 1, 0))
            s_left = jnp.where(lane == 0, 0.0, pltpu.roll(root, 1, 1))
            s_right = jnp.where(lane == col_cells - 1, 0.0, pltpu.roll(root, col_cells - 1, 1))
            p_up = jnp.where(row == 0, 0.0, pltpu.roll(px, 1, 0))
            p_down = jnp.where(row == row_cells - 1, 0.0, pltpu.roll(px, row_cells - 1, 0))
            p_left = jnp.where(lane == 0, 0.0, pltpu.roll(py, 1, 1))
            p_right = jnp.where(lane == col_cells - 1, 0.0, pltpu.roll(py, col_cells - 1, 1))
            total = p_up - p_down + p_left - p_right + ax * (s_up - s_down) + ay * (s_left - s_right)
            main[k, p, 0] = root
            main[k, p, 1] = accel_ref[slot, 0]
            main[k, p, 2] = 0.5 * root * total
            side[k, pl.ds(p, 1), :] = ax[0:1]
            side[k, pl.ds(held + p, 1), :] = ax[row_cells - 1 : row_cells]
            cols = jnp.where(lane == 2 * p, ay[:, 0:1], cols)
            return jnp.where(lane == 2 * p + 1, ay[:, col_cells - 1 : col_cells], cols)

        cols = lax.fori_loop(0, per_owner, one, jnp.zeros((row_cells, col_cells), jnp.float32))
        side[k, 2 * held : 2 * held + row_cells, :] = cols
        side[k, 2 * held + row_cells :, :] = ids_ref[owner]

    side[...] = jnp.zeros_like(side)
    copies = []
    for count, k in enumerate(partner_order(owners)):
        owner = partner(me, k, owners)
        pack(k, owner)
        if count == 0:
            pl.semaphore_wait(barrier, owners - 1)
        for src, dst, send, recv in (
            (main, main_out, main_send, main_recv),
            (side, side_out, side_send, side_recv),
        ):
            copy = pltpu.make_async_remote_copy(
                src_ref=src.at[k],
                dst_ref=dst.at[me],
                send_sem=send.at[k],
                recv_sem=recv.at[k],
                device_id={"yz": owner},
                device_id_type=MESH,
            )
            copy.start()
            copies.append(copy)
    pack(0, me)
    own = [
        pltpu.make_async_copy(main.at[0], main_out.at[me], main_send.at[0]),
        pltpu.make_async_copy(side.at[0], side_out.at[me], side_send.at[0]),
    ]
    for copy in own:
        copy.start()
    for copy in own:
        copy.wait()
    for copy in copies:
        copy.wait()


def side_rows(per_owner):
    return -(-per_owner // 8) * 8


def exchange(source, ids, accel, weight, owners, per_owner):
    slots, _, row_cells, col_cells = accel.shape
    main_shape = (owners, per_owner, 3, row_cells, col_cells)
    side_shape = (owners, 2 * side_rows(per_owner) + row_cells + 8, col_cells)
    return pl.pallas_call(
        functools.partial(exchange_kernel, owners, per_owner),
        out_shape=(
            jax.ShapeDtypeStruct(main_shape, jnp.float32),
            jax.ShapeDtypeStruct(side_shape, jnp.float32),
        ),
        in_specs=[pl.BlockSpec(memory_space=pltpu.SMEM)] + [pl.BlockSpec(memory_space=pltpu.VMEM)] * 3,
        out_specs=(pl.BlockSpec(memory_space=pl.ANY), pl.BlockSpec(memory_space=pl.ANY)),
        scratch_shapes=[
            pltpu.VMEM(main_shape, jnp.float32),
            pltpu.VMEM(side_shape, jnp.float32),
        ]
        + [pltpu.SemaphoreType.DMA((owners,))] * 4,
        compiler_params=pltpu.CompilerParams(
            collective_id=0, has_side_effects=True, vmem_limit_bytes=40 * 2**20
        ),
        name="brick_exchange",
    )(source, ids, accel, weight)


def split(value):
    high = value.astype(jnp.bfloat16)
    return high, (value - high.astype(jnp.float32)).astype(jnp.bfloat16)


def dot32(left, right):
    return jnp.dot(left, right, preferred_element_type=jnp.float32)


def solver_kernel(
    slabs, owners, rows, y_bricks, per_owner,
    from_ref, place_ref, fluid_ref, main_ref, side_ref, fwd_hbm, inv_hbm, table_x, table_xt, inverse_ref, ends_ref, couple_ref,
    solution_ref, residual_ref,
    fwd, inv, root, accel_x, accel_y, accel_z, source, fluid, diagonal, near_root, near_accel, near_t, t_pad,
    res_hl, spec, x_hl, update, image, edge, gathered, part, total_yz, total_gx, relay,
    table_sem, near_sem, row_sem, t_sem, t_row_sem, edge_sem, yz_sem, gx_sem,
):
    g = lax.axis_index("gx")
    z = lax.axis_index("yz")
    barrier = pltpu.get_barrier_semaphore()
    for k in range(1, owners):
        pl.semaphore_signal(barrier, inc=1, device_id={"yz": lax.rem(z + k, owners)}, device_id_type=MESH)
    for k in range(1, slabs):
        pl.semaphore_signal(barrier, inc=1, device_id={"gx": lax.rem(g + k, slabs)}, device_id_type=MESH)

    table_copies = [
        pltpu.make_async_copy(fwd_hbm, fwd, table_sem.at[0]),
        pltpu.make_async_copy(inv_hbm, inv, table_sem.at[1]),
    ]
    for copy in table_copies:
        copy.start()

    has_low, has_high = z > 0, z < owners - 1
    has_prev, has_next = g > 0, g < slabs - 1

    def remote(src, dst, sems, device):
        return pltpu.make_async_remote_copy(
            src_ref=src, dst_ref=dst, send_sem=sems.at[0], recv_sem=sems.at[1],
            device_id=device, device_id_type=MESH,
        )

    half = rows // 2
    middle = owners // 2
    via = (0, owners - 1)
    tiles = NY // TILE

    class Piece:
        def __init__(self, src, near, held, sems):
            parts = [pl.ds(0, half), pl.ds(half, half)]

            def copy(src, dst, send, recv, device):
                return pltpu.make_async_remote_copy(
                    src_ref=src, dst_ref=dst, send_sem=sems.at[send], recv_sem=sems.at[recv],
                    device_id={"yz": device}, device_id_type=MESH,
                )

            self.up = copy(src, near.at[0], 0, 1, jnp.minimum(z + 1, owners - 1))
            self.down = copy(src, near.at[1], 2, 3, jnp.maximum(z - 1, 0))
            self.out = [
                [copy(src.at[parts[h]], held.at[d], 4 + h, 6 + d, via[h]) for h in range(2)]
                for d in range(2)
            ]
            self.on = [
                [copy(held.at[d], near.at[d, parts[h]], 8 + d, 10 + h, middle - d) for h in range(2)]
                for d in range(2)
            ]

        def start(self):
            pl.when((z < owners - 1) & (z != middle - 1))(self.up.start)
            pl.when((z > 0) & (z != middle))(self.down.start)
            for d in range(2):
                for h in range(2):
                    pl.when(z == middle - 1 + d)(self.out[d][h].start)

        def forward(self):
            for h in range(2):
                @pl.when(z == via[h])
                def _():
                    for d in range(2):
                        self.out[d][h].wait_recv()
                        self.on[d][h].start()

        def wait(self):
            @pl.when((z < owners - 1) & (z != middle - 1))
            def _():
                self.up.wait_send()
                self.down.wait_recv()

            @pl.when((z > 0) & (z != middle))
            def _():
                self.down.wait_send()
                self.up.wait_recv()

            for d in range(2):
                @pl.when(z == middle - 1 + d)
                def _():
                    for h in range(2):
                        self.out[d][h].wait_send()
                        self.on[1 - d][h].wait_recv()

            for h in range(2):
                @pl.when(z == via[h])
                def _():
                    for d in range(2):
                        self.on[d][h].wait_send()

    def row_copies(buf, sems):
        after = remote(
            buf.at[pl.ds(rows, PAD)], buf.at[pl.ds(0, PAD)], sems.at[0],
            {"gx": jnp.minimum(g + 1, slabs - 1)},
        )
        before = remote(
            buf.at[pl.ds(PAD, PAD)], buf.at[pl.ds(PAD + rows, PAD)], sems.at[1],
            {"gx": jnp.maximum(g - 1, 0)},
        )
        return after, before

    def start_pair(pair, to_first, to_second):
        @pl.when(to_first)
        def _():
            pair[0].start()

        @pl.when(to_second)
        def _():
            pair[1].start()

    def wait_pair(pair, has_before, has_after):
        @pl.when(has_after)
        def _():
            pair[0].wait_send()
            pair[1].wait_recv()

        @pl.when(has_before)
        def _():
            pair[1].wait_send()
            pair[0].wait_recv()

    def clear_rows(buf):
        @pl.when(jnp.logical_not(has_prev))
        def _():
            buf[pl.ds(0, PAD)] = jnp.zeros((PAD, NY), jnp.float32)

        @pl.when(jnp.logical_not(has_next))
        def _():
            buf[pl.ds(PAD + rows, PAD)] = jnp.zeros((PAD, NY), jnp.float32)

    def clear_planes(near):
        @pl.when(jnp.logical_not(has_low))
        def _():
            near[0] = jnp.zeros((rows, NY), jnp.float32)

        @pl.when(jnp.logical_not(has_high))
        def _():
            near[1] = jnp.zeros((rows, NY), jnp.float32)

    held = side_rows(per_owner)
    per_tile = TILE // B
    brick_row = lax.broadcasted_iota(jnp.int32, (BR, B), 0)
    brick_lane = lax.broadcasted_iota(jnp.int32, (BR, B), 1)

    def place(first, n, carry):
        b = (n // per_tile) * y_bricks + first + n % per_tile
        owner = from_ref[b]
        p = place_ref[b]
        keep = fluid_ref[b]
        r0 = pl.multiple_of((b // y_bricks) * BR, BR)
        c0 = pl.multiple_of((b % y_bricks) * B, B)
        at = (pl.ds(r0, BR), pl.ds(c0, B))
        at_pad = (pl.ds(pl.multiple_of(r0 + PAD, PAD), BR), pl.ds(c0, B))
        root[at_pad] = main_ref[owner, p, 0] * keep
        accel_z[at] = main_ref[owner, p, 1] * keep
        source[at] = main_ref[owner, p, 2] * keep
        top = side_ref[owner, pl.ds(p, 1), :]
        bottom = side_ref[owner, pl.ds(held + p, 1), :]
        cols = side_ref[owner, 2 * held : 2 * held + BR, :]
        begin = jnp.sum(jnp.where(brick_lane == 2 * p, cols, 0.0), axis=1, keepdims=True)
        end = jnp.sum(jnp.where(brick_lane == 2 * p + 1, cols, 0.0), axis=1, keepdims=True)
        accel_x[at_pad] = keep * jnp.where(
            brick_row == 0, top, jnp.where(brick_row == BR - 1, bottom, 0.0)
        )
        accel_y[at] = keep * jnp.where(
            brick_lane == 0, begin, jnp.where(brick_lane == B - 1, end, 0.0)
        )
        fluid[at] = jnp.full((BR, B), keep, jnp.float32)
        return carry

    pieces = []
    for j in range(tiles):
        lax.fori_loop(
            0, rows // BR * per_tile, functools.partial(place, j * per_tile), 0, unroll=2
        )
        if j == 0:
            pl.semaphore_wait(barrier, owners + slabs - 2)
        at = pl.ds(j * TILE, TILE)
        pair = [
            Piece(root.at[pl.ds(PAD, rows), at], near_root.at[:, :, at], relay.at[j], near_sem.at[0, j]),
            Piece(accel_z.at[:, at], near_accel.at[:, :, at], relay.at[tiles + j], near_sem.at[1, j]),
        ]
        for piece in pair:
            piece.start()
        pieces.append(pair)
    row_pairs = [row_copies(root, row_sem.at[0]), row_copies(accel_x, row_sem.at[1])]
    for pair in row_pairs:
        start_pair(pair, has_next, has_prev)
    for buf in (root, accel_x, t_pad.at[0], t_pad.at[1]):
        clear_rows(buf)
    for piece in pieces[0]:
        piece.forward()
    for buf in (near_root, near_accel, near_t.at[0], near_t.at[1]):
        clear_planes(buf)
    for pair in row_pairs:
        wait_pair(pair, has_prev, has_next)

    row = lax.broadcasted_iota(jnp.int32, (CHUNK, NY), 0)
    lane = lax.broadcasted_iota(jnp.int32, (CHUNK, NY), 1)

    def left(value):
        return jnp.where(lane == 0, 0.0, pltpu.roll(value, 1, 1))

    def right(value):
        return jnp.where(lane == NY - 1, 0.0, pltpu.roll(value, NY - 1, 1))

    def at_chunk(i):
        r0 = pl.multiple_of(i * CHUNK, CHUNK)
        return pl.ds(r0, CHUNK), pl.ds(r0, CHUNK + 2 * PAD)

    def shifts(wide):
        return (
            wide[PAD - 1 : PAD - 1 + CHUNK],
            wide[PAD : PAD + CHUNK],
            wide[PAD + 1 : PAD + 1 + CHUNK],
        )

    def store_residual(at, cols, value):
        residual_ref[0, at, cols] = value
        high, low = split(value)
        res_hl[0, at, cols] = high
        res_hl[1, at, cols] = low

    def prepare(i, carry):
        at, wide_at = at_chunk(i)
        s_wide = root[wide_at, :]
        s_up, s, s_down = shifts(s_wide)
        ax_wide = accel_x[wide_at, :]
        ax = ax_wide[PAD : PAD + CHUNK]
        px_up, _, px_down = shifts(s_wide * ax_wide)
        ay = accel_y[at, :]
        py = s * ay
        s_left, s_right = left(s), right(s)
        total = jnp.where(row == 0, px_up + ax * s_up, 0.0)
        total = total - jnp.where(row == CHUNK - 1, px_down + ax * s_down, 0.0)
        total = total + jnp.where(lane % B == 0, left(py) + ay * s_left, 0.0)
        total = total - jnp.where(lane % B == B - 1, right(py) + ay * s_right, 0.0)
        source[at, :] = source[at, :] + 0.5 * s * total
        ring = s_up + s_down + s_left + s_right
        diagonal[at, :] = s * (shift_rate * s + ring) + (1.0 - fluid[at, :])
        return carry

    chunks = rows // CHUNK
    lax.fori_loop(0, chunks, prepare, 0)
    for pair in pieces[1:]:
        for piece in pair:
            piece.forward()
    for copy in table_copies:
        copy.wait()

    every = pl.ds(0, NY)

    def add_planes(cols, i, carry):
        at, _ = at_chunk(i)
        s = root[pl.ds(pl.multiple_of(i * CHUNK + PAD, PAD), CHUNK), cols]
        s_low, s_high = near_root[0, at, cols], near_root[1, at, cols]
        total = s_low * near_accel[0, at, cols] - s_high * near_accel[1, at, cols]
        total = total + accel_z[at, cols] * (s_low - s_high)
        store_residual(at, cols, source[at, cols] + 0.5 * s * total)
        diagonal[at, cols] = diagonal[at, cols] + s * (s_low + s_high)
        return carry

    def three(left_hl, right_hl):
        lh, ll = left_hl
        rh, rl = right_hl
        return dot32(lh, rh) + dot32(lh, rl) + dot32(ll, rh)

    def tile_at(j):
        return pl.ds(pl.multiple_of(j * WIDE, WIDE), WIDE)

    def accumulate(j):
        cols = pl.ds(j * TILE, TILE)

        def one(k, carry):
            at = tile_at(k)
            lines = three((res_hl[0, :, cols], res_hl[1, :, cols]), (fwd[0, cols, at], fwd[1, cols, at]))
            if j:
                lines = spec[:, at] + lines
            spec[:, at] = lines
            return carry

        lax.fori_loop(0, NY // WIDE, one, 0)

    def precondition(it):
        def forward(j, carry):
            at = tile_at(j)
            if it:
                lines = three((res_hl[0], res_hl[1]), (fwd[0, :, at], fwd[1, :, at]))
            else:
                lines = spec[:, at]
            modes = three((table_x[0], table_x[1]), split(lines)) * inverse_ref[:, at]
            spec[:, at] = modes
            edge[it, 0:1, at] = jnp.sum(modes * ends_ref[:, 0:1], axis=0, keepdims=True)
            edge[it, 1:2, at] = jnp.sum(modes * ends_ref[:, B : B + 1], axis=0, keepdims=True)
            return carry

        edge[it] = jnp.zeros((8, NY), jnp.float32)
        lax.fori_loop(0, NY // WIDE, forward, 0)
        copies = [
            remote(edge.at[it], gathered.at[it, g], edge_sem.at[it, k], {"gx": lax.rem(g + k, slabs)})
            for k in range(1, slabs)
        ]
        for copy in copies:
            copy.start()
        gathered[it, g] = edge[it]
        for copy in copies:
            copy.wait()
        sides = []
        for side in range(2):
            total = jnp.zeros((1, NY), jnp.float32)
            for j in range(slabs):
                for end in range(2):
                    n = 2 * j + end
                    total = total + couple_ref[g, side, n : n + 1, :] * gathered[it, j, end : end + 1, :]
            sides.append(total)
        edge_y = jnp.concatenate(sides, axis=0)
        part[0:2, :] = edge_y

        def back_x(j, carry):
            at = tile_at(j)
            fix = ends_ref[:, 0:1] * part[0:1, at] + ends_ref[:, B : B + 1] * part[1:2, at]
            modes = spec[:, at] + inverse_ref[:, at] * fix
            high, low = split(three((table_xt[0], table_xt[1]), split(modes)))
            x_hl[0, :, at] = high
            x_hl[1, :, at] = low
            return carry

        lax.fori_loop(0, NY // WIDE, back_x, 0)
        pairs = []
        for j in range(tiles):
            at = pl.ds(j * TILE, TILE)
            out = three((x_hl[0], x_hl[1]), (inv[0, :, at], inv[1, :, at])) * fluid[:, at]
            update[it, :, at] = out
            t_pad[it, pl.ds(PAD, rows), at] = out * root[pl.ds(PAD, rows), at]
            piece = Piece(
                t_pad.at[it, pl.ds(PAD, rows), at], near_t.at[it, :, :, at],
                relay.at[(2 + it) * tiles + j], t_sem.at[it, j],
            )
            piece.start()
            pairs.append(piece)
        rim = row_copies(t_pad.at[it], t_row_sem.at[it])
        start_pair(rim, has_next, has_prev)
        pairs[0].forward()
        wait_pair(rim, has_prev, has_next)
        return pairs

    def operate(it, pairs):
        def within(i, carry):
            at, wide_at = at_chunk(i)
            t_up, t, t_down = shifts(t_pad[it, wide_at, :])
            _, s, _ = shifts(root[wide_at, :])
            near = t_up + t_down + left(t) + right(t)
            image[it, at, :] = diagonal[at, :] * update[it, at, :] - s * near
            return carry

        lax.fori_loop(0, chunks, within, 0)
        for piece in pairs[1:]:
            piece.forward()

        def across(cols, i, carry):
            energy, curve = carry
            at, _ = at_chunk(i)
            s = root[pl.ds(pl.multiple_of(i * CHUNK + PAD, PAD), CHUNK), cols]
            u = update[it, at, cols]
            out = image[it, at, cols] - s * (near_t[it, 0, at, cols] + near_t[it, 1, at, cols])
            image[it, at, cols] = out
            return energy + u * residual_ref[0, at, cols], curve + u * out

        zero = jnp.zeros((CHUNK, TILE), jnp.float32)
        energy, curve = zero, zero
        for j in range(tiles):
            pairs[j].wait()
            energy, curve = lax.fori_loop(
                0, chunks, functools.partial(across, pl.ds(j * TILE, TILE)), (energy, curve)
            )
        part_row = lax.broadcasted_iota(jnp.int32, (8, B), 0)
        block = jnp.where(part_row < 4, jnp.sum(energy), jnp.sum(curve))
        for buf, sems, axis, count, index in (
            (total_yz, yz_sem, "yz", owners, z),
            (total_gx, gx_sem, "gx", slabs, g),
        ):
            buf[it, index] = block
            copies = [
                remote(buf.at[it, index], buf.at[it, index], sems.at[it, k], {axis: lax.rem(index + k, count)})
                for k in range(1, count)
            ]
            for copy in copies:
                copy.start()
            for copy in copies:
                copy.wait()
            block = buf[it, 0]
            for k in range(1, count):
                block = block + buf[it, k]
        return block[0:1, 0:1], block[4:5, 0:1]

    for j in range(tiles):
        for piece in pieces[j]:
            piece.wait()
        lax.fori_loop(0, chunks, functools.partial(add_planes, pl.ds(j * TILE, TILE)), 0)
        accumulate(j)
    energy_now, curvature = operate(0, precondition(0))
    step_now = energy_now / curvature

    def advance(i, carry):
        at, _ = at_chunk(i)
        store_residual(at, every, residual_ref[0, at, :] - step_now * image[0, at, :])
        return carry

    lax.fori_loop(0, chunks, advance, 0)
    energy_next, curvature = operate(1, precondition(1))
    beta = energy_next / energy_now
    step_next = energy_next / (curvature - beta * energy_next / step_now)

    def finish(i, carry):
        at, _ = at_chunk(i)
        first, second = update[0, at, :], update[1, at, :]
        solution_ref[0, at, :] = step_now * first + step_next * (second + beta * first)
        residual_ref[0, at, :] = residual_ref[0, at, :] - step_next * (
            image[1, at, :] + beta * image[0, at, :]
        )
        return carry

    lax.fori_loop(0, chunks, finish, 0)


def solve(owner_of, place_of, fluid, main, side, slabs, owners, rows, y_bricks):
    tables = [jnp.asarray(t) for t in solver_tables(slabs, rows)]
    plane = (rows, NY)
    padded = (rows + 2 * PAD, NY)
    f32, bf16 = jnp.float32, jnp.bfloat16
    vmem = pl.BlockSpec(memory_space=pltpu.VMEM)
    smem = pl.BlockSpec(memory_space=pltpu.SMEM)
    hbm = pl.BlockSpec(memory_space=pl.ANY)
    dma = pltpu.SemaphoreType.DMA
    out = jax.ShapeDtypeStruct((1,) + plane, f32)
    return pl.pallas_call(
        functools.partial(solver_kernel, slabs, owners, rows, y_bricks, main.shape[1]),
        out_shape=(out, out),
        in_specs=[smem] * 3 + [vmem, vmem, hbm, hbm] + [vmem] * 5,
        out_specs=(vmem, vmem),
        scratch_shapes=[
            pltpu.VMEM((2, NY, NY), bf16),
            pltpu.VMEM((2, NY, NY), bf16),
            pltpu.VMEM(padded, f32),
            pltpu.VMEM(padded, f32),
            pltpu.VMEM(plane, f32),
            pltpu.VMEM(plane, f32),
            pltpu.VMEM(plane, f32),
            pltpu.VMEM(plane, f32),
            pltpu.VMEM(plane, f32),
            pltpu.VMEM((2,) + plane, f32),
            pltpu.VMEM((2,) + plane, f32),
            pltpu.VMEM((ITERS, 2) + plane, f32),
            pltpu.VMEM((ITERS,) + padded, f32),
            pltpu.VMEM((2,) + plane, bf16),
            pltpu.VMEM(plane, f32),
            pltpu.VMEM((2,) + plane, bf16),
            pltpu.VMEM((ITERS,) + plane, f32),
            pltpu.VMEM((ITERS,) + plane, f32),
            pltpu.VMEM((ITERS, 8, NY), f32),
            pltpu.VMEM((ITERS, slabs, 8, NY), f32),
            pltpu.VMEM((8, NY), f32),
            pltpu.VMEM((ITERS, owners, 8, B), f32),
            pltpu.VMEM((ITERS, slabs, 8, B), f32),
            pltpu.VMEM(((2 + ITERS) * (NY // TILE), 2, rows // 2, TILE), f32),
            dma((2,)),
            dma((2, NY // TILE, 12)),
            dma((2, 2, 2)),
            dma((ITERS, NY // TILE, 12)),
            dma((ITERS, 2, 2)),
            dma((ITERS, slabs, 2)),
            dma((ITERS, owners, 2)),
            dma((ITERS, slabs, 2)),
        ],
        compiler_params=pltpu.CompilerParams(
            collective_id=1, has_side_effects=True, vmem_limit_bytes=45 * 2**20
        ),
        name="pressure_solver",
    )(owner_of, place_of, fluid, main, side, *tables)


def deliver_kernel(solution_in, residual_in, solution_ref, residual_ref):
    solution_ref[...] = solution_in[...]
    residual_ref[...] = residual_in[...]


def deliver(values):
    _, rows, cols = values[0].shape
    steps = 4
    block = pl.BlockSpec((1, rows // steps, cols), lambda i: (0, i, 0))
    return pl.pallas_call(
        deliver_kernel,
        grid=(steps,),
        out_shape=tuple(jax.ShapeDtypeStruct(v.shape, v.dtype) for v in values),
        in_specs=[block, block],
        out_specs=(block, block),
        name="deliver",
    )(*values)


def ranks_of(owners_of, owner_count):
    one_hot = (owners_of[..., None] == jnp.arange(owner_count, dtype=jnp.int32)).astype(jnp.int32)
    earlier = jnp.cumsum(one_hot, axis=-2) - one_hot
    return jnp.sum(earlier * one_hot, axis=-1)


def on_device(camera_accel, camera_weight, brick_slot, brick_solid):
    owner_count = lax.axis_size("yz")
    slabs = lax.axis_size("gx")
    slot_count = brick_slot.shape[1]
    per_owner = 3 * slot_count // (2 * owner_count)
    rows = NX // slabs
    y_bricks = NY // B
    slots = jnp.arange(slot_count, dtype=jnp.int32)

    brick_ids = brick_slot[0]
    owners_of = brick_ids // slot_count
    target = owners_of * per_owner + ranks_of(owners_of, owner_count)
    positions = jnp.arange(owner_count * per_owner, dtype=jnp.int32)
    matches = target[None, :] == positions[:, None]
    source = jnp.sum(jnp.where(matches, slots[None, :], 0), axis=1)

    found = jnp.sum(jnp.where(matches, 1 + brick_ids[None, :] % slot_count, 0), axis=1) - 1
    ids = jnp.pad(
        found.astype(jnp.float32).reshape(owner_count, 1, per_owner),
        ((0, 0), (0, 7), (0, B - per_owner)),
        constant_values=-1.0,
    )
    main, side = exchange(source, ids, camera_accel[0], camera_weight[0], owner_count, per_owner)
    held_ids = side[:, -8, :per_owner].reshape(-1)
    arrived = held_ids[None, :] == slots.astype(jnp.float32)[:, None]
    anchor = jnp.sum(jnp.where(arrived, positions[None, :], 0), axis=1)
    fluid = (1 - brick_solid[0]).astype(jnp.float32)
    values = solve(
        anchor // per_owner, anchor % per_owner, fluid, main, side, slabs, owner_count, rows, y_bricks
    )
    return deliver(values)


def solution(mesh):
    return jax.shard_map(
        on_device,
        mesh=mesh,
        in_specs=(
            P("gx", "yz", None, None, None),
            P("gx", "yz", None, None),
            P("gx", "yz"),
            P("gx", "yz"),
        ),
        out_specs=(P("yz", "gx", None), P("yz", "gx", None)),
        check_vma=False,
    )
```
